256 devices in a mesh: row: 32 (over z_hi, y, core), col: 8 (over z_lo, x).
Axes of the slice: x: 4, y: 4, z: 8 (z_hi: 4, z_lo: 2; z = z_hi * 2 + z_lo), core: 2. Of those that a mesh axis runs over, the one named last changes fastest.
Arguments:
- holograms: float32 [4, 4096, 4096], P(None, 'row', 'col'), may hold values from -6 to 6
- fresnel: float32 [4], replicated, may hold values from 0.01 to 0.05
- ctf_terms: float32 [2], replicated, may hold values from 0.1 to 0.6
Outputs:
- phase: float32 [4096, 4096], P('row', 'col')
The draws below stay inside these ranges and needn't reach their ends.
All inputs are finite; a program needn't handle non-finite values.
Results may differ from the reference program's by a relative error of at most 0.0003.
Values sent between devices are 32-bit elements; how exact they have to be, the bound alone decides.
No kernel may reach another device: no remote copies, remote signals or barrier semaphores. Data moves between devices by JAX's collectives and lax.ppermute only.
A program may use at most 128 MiB of HBM per device.

```python
import math
import jax
import jax.numpy as jnp

N = 4096
NDIST = 4


def block_scale(own_key, shape, shards, low, high):
    gain, own = 1.0, jax.random.fold_in(own_key, 6)
    for position, parts in shards:
        steps = jnp.exp(jax.random.uniform(jax.random.fold_in(own, position), (parts,), jnp.float32, low / len(shards), high / len(shards)))
        gain = gain * jnp.repeat(steps, shape[position] // parts).reshape([-1 if axis == position else 1 for axis in range(len(shape))])
    return gain


def centred(stream_key, dims, width, bound, split=(), held_as=jnp.bfloat16):
    level = block_scale(stream_key, dims, split, -0.22, 0.18) if split else 1.0
    array = jax.random.normal(stream_key, dims, jnp.float32) * width * level
    return jnp.minimum(jnp.maximum(array, -bound), bound).astype(held_as)


def setup_inputs(seed: int = 0) -> dict:
    key_of = jax.random.split(jax.random.key(seed), 4)
    return {
        "holograms": centred(key_of[0], (NDIST, N, N), 1.0, 6.0, ((1, 32), (2, 8)), jnp.float32),
        "fresnel": jnp.clip(jnp.exp(jax.random.uniform(key_of[1], (NDIST,), jnp.float32, math.log(0.01), math.log(0.05))), 0.01, 0.05),
        "ctf_terms": jnp.clip(jax.random.uniform(key_of[2], (2,), jnp.float32, 0.1, 0.6), 0.1, 0.6),
    }


def reference(holograms, fresnel, ctf_terms):
    indices = jnp.arange(N, dtype=jnp.int32)
    signed = jnp.where(2 * indices >= N, indices - N, indices)
    squares = signed * signed
    squared_radius = (squares[:, None] + squares[None, :]).astype(jnp.float32)
    freq_scale = math.pi / (N * N)
    numerator = None
    denominator = None
    for member in range(NDIST):
        chirp_phase = squared_radius * freq_scale / fresnel[member]
        weight = 2.0 * (jnp.sin(chirp_phase) + ctf_terms[0] * jnp.cos(chirp_phase))
        term = weight * jnp.fft.fft2(holograms[member])
        if member == 0:
            numerator = term
            denominator = weight * weight
        else:
            numerator = numerator + term
            denominator = denominator + weight * weight
    retrieved = numerator / (denominator + ctf_terms[1])
    return jnp.real(jnp.fft.ifft2(retrieved)).astype(jnp.float32)
```

```python
import math

import jax
import jax.numpy as jnp
import ml_dtypes
import numpy as np
from jax import lax
from jax.experimental import pallas as pl
from jax.experimental.pallas import tpu as pltpu
from jax.sharding import PartitionSpec as P

N = 4096
POS, NEG, ZERO, HALF = range(4)
F32 = jnp.float32
BF16 = jnp.bfloat16


def residues(quad):
    low, high = 2 * quad, 2 * quad + 1
    if quad == 0:
        return [0, 1, 16, 31]
    return [low, high, 32 - low, 32 - high]


def member(kind, group, slot):
    if kind == POS:
        return 4 * group + slot
    if kind == NEG:
        return 127 - 4 * group - slot
    if kind == ZERO:
        return [2 * group, 2 * group + 1, 128 - 2 * group if group else 64, 127 - 2 * group][slot]
    return [2 * group, 2 * group + 1, 127 - 2 * group, 126 - 2 * group][slot]


def halves(matrix):
    high = matrix.astype(ml_dtypes.bfloat16)
    low = (matrix - high.astype(np.float64)).astype(ml_dtypes.bfloat16)
    return np.stack([high, low])


def turn(product, length):
    angle = 2.0 * np.pi * (np.asarray(product, np.int64) % length) / length
    return np.cos(angle), np.sin(angle)


def row_constants():
    mats = []
    for kind in range(4):
        k2 = np.array([[member(kind, g, s) for s in range(4)] for g in range(32)])
        cosine, sine = turn(k2[:, :, None] * np.arange(128), 128)
        real = np.concatenate([cosine, sine], -1)
        imag = np.concatenate([-sine, cosine], -1)
        both = np.stack([real.reshape(32, 2, 2, 256), imag.reshape(32, 2, 2, 256)], 2)
        mats.append(halves(both.reshape(256, 256)))
    twist = np.stack(turn(np.arange(32)[:, None] * np.arange(128), N)).astype(np.float32)
    return np.stack(mats), twist


def column_constants():
    cosine, sine = turn(np.arange(16)[:, None] * np.arange(16), 16)
    eye8 = np.eye(8)
    forward = np.block(
        [
            [np.kron(eye8, cosine), np.kron(eye8, -sine)],
            [np.kron(eye8, sine), np.kron(eye8, cosine)],
        ]
    )
    pick = np.kron(np.eye(4), np.ones((2, 1)))
    twice = np.ones((1, 2))

    def spread(block):
        return np.kron(twice, np.kron(pick, block))

    inverse = np.block([[spread(cosine), spread(sine)], [spread(-sine), spread(cosine)]])
    lane = np.arange(128)
    within = lane % 16
    top = lane // 64
    step = np.arange(128)[None, :, None] + 128 * np.arange(2)[:, None, None]
    ahead = np.stack(turn(step * within, N)).astype(np.float32)
    step = np.arange(64)[None, :, None] + 128 * np.arange(2)[:, None, None] + 64 * top
    behind = np.stack(turn(step * within, N)).astype(np.float32)
    step = np.arange(2)[:, None, None] + 2 * top
    spin = np.stack(turn(step * np.arange(64)[None, :, None], 256)).astype(np.float32)
    return halves(forward), halves(inverse), ahead, np.stack([behind, spin])


def image_constants():
    mats = []
    for kind in range(4):
        k2 = np.array([[member(kind, g, s) for g in range(32)] for s in range(4)])
        k2 = k2.reshape(2, 2, 32).transpose(0, 2, 1).reshape(2, 64)
        cosine, sine = turn(np.arange(128)[:, None, None] * k2, 128)
        real = np.stack([cosine, -sine], 2).reshape(128, 256)
        imag = np.stack([sine, cosine], 2).reshape(128, 256)
        mats.append(halves(np.concatenate([real, imag])))
    lane = np.arange(256)
    quad = 4 * (lane // 128) + 2 * (lane // 64 % 2) + lane // 8 % 2
    k1 = np.array([residues(q)[s] for q, s in zip(quad, lane // 16 % 4)])
    twist = np.stack(turn(np.arange(128)[:, None] * k1, N)).astype(np.float32)
    cosine, sine = turn(np.arange(32)[:, None] * k1, 32)
    same = (np.arange(8)[:, None] == lane % 8).astype(np.float64)
    real = np.concatenate([cosine[:, None] * same, -sine[:, None] * same], -1)
    imag = np.concatenate([sine[:, None] * same, cosine[:, None] * same], -1)
    last = np.concatenate([real, imag], 1).reshape(512, 512) * (0.5 / (N * N))
    return np.stack(mats), twist, halves(last)


def turned(value, angle_index, length, sign):
    angle_index %= length
    real, imag = value
    if angle_index == 0:
        return value
    if 4 * angle_index == length:
        return (-imag, real) if sign > 0 else (imag, -real)
    if 2 * angle_index == length:
        return (-real, -imag)
    if 4 * angle_index == 3 * length:
        return (imag, -real) if sign > 0 else (-imag, real)
    angle = sign * 2.0 * math.pi * angle_index / length
    cosine, sine = math.cos(angle), math.sin(angle)
    if (8 * angle_index) % length == 0:
        scale = abs(cosine)
        plus, minus = (real + imag) * scale, (real - imag) * scale
        if cosine > 0:
            return (minus, plus) if sine > 0 else (plus, -minus)
        return (-plus, minus) if sine > 0 else (-minus, -plus)
    return (real * cosine - imag * sine, imag * cosine + real * sine)


def plus(a, b):
    return (a[0] + b[0], a[1] + b[1])


def minus(a, b):
    return (a[0] - b[0], a[1] - b[1])


def transform(values, sign):
    length = len(values)
    if length == 1:
        return values
    if length == 2:
        return [plus(values[0], values[1]), minus(values[0], values[1])]
    quarter = length // 4
    columns = []
    for b in range(quarter):
        z0, z1, z2, z3 = (values[a * quarter + b] for a in range(4))
        even, odd = plus(z0, z2), plus(z1, z3)
        even_gap, odd_gap = minus(z0, z2), turned(minus(z1, z3), 1, 4, sign)
        outs = [plus(even, odd), plus(even_gap, odd_gap), minus(even, odd), minus(even_gap, odd_gap)]
        columns.append([turned(z, b * k, length, sign) for k, z in enumerate(outs)])
    result = [None] * length
    for k in range(4):
        for m, z in enumerate(transform([columns[b][k] for b in range(quarter)], sign)):
            result[k + 4 * m] = z
    return result


def times(value, cosine, sine):
    real, imag = value
    return (real * cosine - imag * sine, imag * cosine + real * sine)


def split(value):
    high = value.astype(BF16)
    return high, (value - high.astype(F32)).astype(BF16)


def product(left, right, dims):
    def one(a, b):
        return lax.dot_general(a, b, (dims, ((), ())), preferred_element_type=F32)

    return one(left[0], right[0]) + (one(left[0], right[1]) + one(left[1], right[0]))


def rows_kernel(field_ref, mats_ref, twist_ref, out_ref, high_ref, low_ref):
    for j in range(2):
        lines = []
        for n1 in range(32):
            at = pl.ds(128 * (n1 % 4), 128)
            lines.append(
                (field_ref[n1 // 4, 2 * j, :, at], field_ref[n1 // 4, 2 * j + 1, :, at])
            )
        lines = transform(lines, -1)
        for quad in range(8):
            for slot, k1 in enumerate(residues(quad)):
                line = lines[k1]
                if k1:
                    line = times(line, twist_ref[0, pl.ds(k1, 1), :], -twist_ref[1, pl.ds(k1, 1), :])
                rows = pl.ds(128 * quad + 32 * slot + 16 * j, 16)
                for part in range(2):
                    high, low = split(line[part])
                    high_ref[rows, pl.ds(128 * part, 128)] = high
                    low_ref[rows, pl.ds(128 * part, 128)] = low
    lane = lax.broadcasted_iota(jnp.int32, (256, 128), 1)
    for pair in range(4):
        rows = pl.ds(256 * pair, 256)
        data = (high_ref[rows, :], low_ref[rows, :])

        def mixed(kind):
            return product((mats_ref[kind, 0], mats_ref[kind, 1]), data, ((1,), (1,)))

        low_half, high_half = mixed(POS), mixed(NEG)
        if pair == 0:
            zero, half = mixed(ZERO), mixed(HALF)
        for side in range(2):
            at = slice(128 * side, 128 * side + 128)
            block = jnp.where(lane < 64, low_half[:, at], high_half[:, at])
            if pair == 0 and side == 0:
                block = jnp.where(lane < 32, zero[:, at], block)
                block = jnp.where((lane >= 64) & (lane < 96), half[:, at], block)
            out_ref[pl.ds(64 * pair + 32 * side, 32)] = block.reshape(32, 8, 128)


def sine_turns(turns):
    t = turns - jnp.round(turns)
    square = t * t
    total = SINE[-1]
    for coefficient in SINE[-2::-1]:
        total = total * square + coefficient
    return total * t


def sine_fit():
    nodes = np.cos(np.pi * (np.arange(400) + 0.5) / 800) * 0.5
    basis = np.stack([nodes ** (2 * k + 1) for k in range(8)], 1)
    return [float(c) for c in np.linalg.lstsq(basis, np.sin(2 * np.pi * nodes), rcond=None)[0]]


SINE = sine_fit()


def device_number():
    return 8 * lax.axis_index("row") + lax.axis_index("col")


def columns_kernel(
    params_ref, field_ref, forward_ref, inverse_ref, ahead_ref, behind_ref, out_ref, work_ref, back_ref
):
    device = device_number()
    quad, group = device // 32, device % 32
    sub = lax.broadcasted_iota(jnp.int32, (8, 128), 0)
    lane = lax.broadcasted_iota(jnp.int32, (8, 128), 1)
    first = (sub & 2) == 0
    sign = jnp.where(first, 1.0, -1.0).astype(F32)
    side = jnp.where(lane < 64, 1.0, -1.0).astype(F32)

    def shift(value, amount, axis):
        return pltpu.roll(value, amount, axis + value.ndim - 2)

    def swap_pairs(value):
        return jnp.where(first, shift(value, 6, 0), shift(value, 2, 0))

    for nb in range(8):
        lines = []
        for na in range(16):
            n = 8 * na + nb
            one, two = field_ref[2 * n], field_ref[2 * n + 1]
            lines.append(
                (jnp.where(first, one, shift(two, 2, 0)), jnp.where(first, shift(one, 6, 0), two))
            )
        for ka, line in enumerate(transform(lines, -1)):
            real, imag = turned(line, nb * ka, 128, -1)
            work_ref[0, ka, nb] = real
            work_ref[1, ka, nb] = imag

    slot = lane >> 5
    s = ((sub >> 2) << 1) | (sub & 1)
    positive = 4 * group + s
    base = 2 * group + (s & 1)
    mirrored = jnp.where(s < 2, base, jnp.where(base == 0, 64, 128 - base))
    halfway = jnp.where(s < 2, base, 127 - base)
    k2 = jnp.where(slot < 2, positive, 127 - positive)
    k1 = 2 * quad + (slot & 1)
    k1 = jnp.where(slot < 2, k1, 32 - k1)
    special = (quad == 0) & ((slot & 1) == 0)
    k2 = jnp.where(special, jnp.where(slot == 0, mirrored, halfway), k2)
    k1 = jnp.where(special, jnp.where(slot == 0, 0, 16), k1)
    v = k1 + 32 * k2
    v = jnp.where(v >= N // 2, v - N, v).astype(F32)
    v_square = v * v
    a2 = lane & 15
    u_base = (64 * (sub & 2) + 256 * a2 - jnp.where(a2 >= 8, N, 0)).astype(F32)
    later = (lane & 16) != 0
    rate_even = jnp.where(later, params_ref[2], params_ref[0])
    rate_odd = jnp.where(later, params_ref[3], params_ref[1])
    offset, gain, floor = params_ref[4], params_ref[5], params_ref[6]

    def rows_of(table, which, start, count, stride):
        picked = []
        for part in range(2):
            tiles = []
            for k in range(count):
                at = pl.ds(start + stride * k, 1)
                upper = jnp.broadcast_to(table[which + (part, 0, at)], (8, 128))
                lower = jnp.broadcast_to(table[which + (part, 1, at)], (8, 128))
                tiles.append(jnp.where(first, upper, lower))
            picked.append(jnp.stack(tiles))
        return picked

    forward = (forward_ref[0], forward_ref[1])
    inverse = (inverse_ref[0], inverse_ref[1])
    natural = ((1,), (0,))
    for bunch in range(4):
        reals, imags = [], []
        for ka in range(4 * bunch, 4 * bunch + 4):
            lines = transform([(work_ref[0, ka, nb], work_ref[1, ka, nb]) for nb in range(8)], -1)
            turned_lines = []
            for kb, line in enumerate(lines):
                angle = 2.0 * math.pi * (ka + 16 * kb) / 256
                line = times(
                    line,
                    jnp.where(first, 1.0, math.cos(angle)).astype(F32),
                    jnp.where(first, 0.0, -math.sin(angle)).astype(F32),
                )
                turned_lines.append(tuple(swap_pairs(z) + sign * z for z in line))
            real = jnp.stack([z[0] for z in turned_lines])
            imag = jnp.stack([z[1] for z in turned_lines])
            cosine, sine = rows_of(ahead_ref, (), ka, 8, 16)
            real, imag = times((real, imag), cosine, -sine)
            reals.append(real.reshape(64, 128))
            imags.append(imag.reshape(64, 128))
        mixed = jnp.concatenate(
            [jnp.concatenate(reals, 0), jnp.concatenate(imags, 0)], 1
        )
        mixed = product(split(mixed), forward, natural)
        reals, imags = [], []
        for step in range(4):
            ka = 4 * bunch + step
            rows = slice(64 * step, 64 * step + 64)
            real = mixed[rows, :128].reshape(8, 8, 128)
            imag = mixed[rows, 128:].reshape(8, 8, 128)
            w1 = ka + 16 * lax.broadcasted_iota(jnp.int32, (8, 8, 128), 0)
            u = u_base + w1.astype(F32)
            radius = u * u + v_square
            even = gain * sine_turns(radius * rate_even + offset)
            odd = gain * sine_turns(radius * rate_odd + offset)
            energy = even * even + odd * odd
            other = jnp.where(later, shift(energy, 16, 1), shift(energy, 112, 1))
            scale = 1.0 / (energy + other + floor)
            reals.append(((even * real + odd * imag) * scale).reshape(64, 128))
            imags.append(((even * imag - odd * real) * scale).reshape(64, 128))
        mixed = jnp.concatenate(
            [jnp.concatenate(reals, 0), jnp.concatenate(imags, 0)], 1
        )
        mixed = product(split(mixed), inverse, natural)
        for step in range(4):
            ka = 4 * bunch + step
            rows = slice(64 * step, 64 * step + 64)
            real = mixed[rows, :128].reshape(8, 8, 128)
            imag = mixed[rows, 128:].reshape(8, 8, 128)
            real = jnp.where(lane < 64, real[:4], real[4:])
            imag = jnp.where(lane < 64, imag[:4], imag[4:])
            cosine, sine = rows_of(behind_ref, (0,), ka, 4, 16)
            real, imag = times((real, imag), cosine, sine)
            real, imag = (swap_pairs(z) + sign * z for z in (real, imag))
            corner = (lane >= 64) & jnp.logical_not(first)
            real, imag = jnp.where(corner, -imag, real), jnp.where(corner, real, imag)
            real, imag = (shift(z, 64, 1) + side * z for z in (real, imag))
            cosine, sine = rows_of(behind_ref, (1,), ka, 4, 16)
            real, imag = times((real, imag), cosine, sine)
            back_ref[0, ka] = real
            back_ref[1, ka] = imag

    for wb in range(8):
        lines = [
            tuple(back_ref[part, wb + 8 * (wa % 2), wa // 2] for part in range(2)) for wa in range(8)
        ]
        for na, line in enumerate(transform(lines, 1)):
            real, imag = turned(line, wb * na, 64, 1)
            work_ref[0, na, wb] = real
            work_ref[1, na, wb] = imag
    bit5 = (lane & 32) != 0
    reflected = (quad == 0) & ((lane & 16) == 0)
    itself = (quad == 0) & (group == 0) & ((lane & 48) == 0) & ((sub & 1) == 0)
    low_half = (lane & 8) == 0
    straight = ((sub & 4) != 0) == (lane >= 64)

    def partner(value):
        across = jnp.where(bit5, shift(value, 32, 1), shift(value, 96, 1))
        down = jnp.where(itself, value, shift(value, 4, 0))
        return jnp.where(reflected, down, across)

    for na in range(8):
        lines = [(work_ref[0, na, wb], work_ref[1, na, wb]) for wb in range(8)]
        for nb, (real, imag) in enumerate(transform(lines, 1)):
            real, imag = real + partner(real), imag - partner(imag)
            packed = real + jnp.where(low_half, -shift(imag, 120, 1), shift(imag, 8, 1))
            crossed = shift(shift(packed, 64, 1), 4, 0)
            out_ref[na + 8 * nb] = jnp.where(straight, packed, crossed)


def image_kernel(field_ref, mats_ref, twist_ref, last_ref, out_ref):
    lane = lax.broadcasted_iota(jnp.int32, (64, 128), 1)
    bit6, bit3 = (lane & 64) != 0, (lane & 8) != 0
    blocks = []
    for pair in range(2):
        tiles = [field_ref[pl.ds(256 * pair + 64 * q, 64), :] for q in range(4)]
        parts = []
        for qb in range(2):
            one, two = tiles[qb], tiles[2 + qb]
            parts.append(
                (
                    jnp.where(bit6, pltpu.roll(two, 64, 1), one),
                    jnp.where(bit6, two, pltpu.roll(one, 64, 1)),
                )
            )
        stacked = []
        for s1 in range(2):
            one, two = parts[0][s1], parts[1][s1]
            stacked.append(jnp.where(bit3, pltpu.roll(two, 8, 1), one))
            stacked.append(jnp.where(bit3, two, pltpu.roll(one, 120, 1)))
        blocks.append(jnp.concatenate(stacked, 0))
    data = split(jnp.concatenate(blocks, 1))

    def mixed(kind):
        return product((mats_ref[kind, 0], mats_ref[kind, 1]), data, ((1,), (0,)))

    lane = lax.broadcasted_iota(jnp.int32, (256, 256), 1)
    value = jnp.where((lane & 32) == 0, mixed(POS), mixed(NEG))
    value = jnp.where((lane & (128 + 64 + 32 + 16 + 8)) == 0, mixed(ZERO), value)
    value = jnp.where((lane & (128 + 64 + 32 + 16 + 8)) == 32, mixed(HALF), value)
    real, imag = times((value[:128], value[128:]), twist_ref[0], twist_ref[1])
    lines = split(jnp.concatenate([real, imag], 1))
    image = product((last_ref[0], last_ref[1]), lines, ((1,), (1,)))
    for n1 in range(32):
        out_ref[n1 // 4, :, pl.ds(128 * (n1 % 4), 128)] = image[16 * n1 : 16 * n1 + 16]


def call(kernel, out_shape, scratch, arguments, scalars=0):
    in_specs = [
        pl.BlockSpec(memory_space=pltpu.SMEM if k < scalars else pltpu.VMEM)
        for k in range(len(arguments))
    ]
    return pl.pallas_call(
        kernel,
        out_shape=jax.ShapeDtypeStruct(out_shape, F32),
        in_specs=in_specs,
        out_specs=pl.BlockSpec(memory_space=pltpu.VMEM),
        scratch_shapes=scratch,
        compiler_params=pltpu.CompilerParams(vmem_limit_bytes=40 * 1024 * 1024),
    )(*arguments)


def image_rows(field):
    mats, twist = row_constants()
    scratch = [pltpu.VMEM((1024, 256), BF16), pltpu.VMEM((1024, 256), BF16)]
    return call(rows_kernel, (256, 8, 128), scratch, [field, jnp.asarray(mats), jnp.asarray(twist)])


def filter_columns(field, fresnel, ctf_terms):
    ratio, regular = ctf_terms[0], ctf_terms[1]
    params = jnp.concatenate(
        [
            1.0 / (2.0 * N * N * fresnel),
            jnp.stack(
                [
                    jnp.arctan(ratio) * (0.5 / math.pi),
                    2.0 * jnp.sqrt(1.0 + ratio * ratio),
                    regular,
                    regular,
                ]
            ),
        ]
    )
    constants = [jnp.asarray(c) for c in column_constants()]
    scratch = [pltpu.VMEM((2, 16, 8, 8, 128), F32), pltpu.VMEM((2, 16, 4, 8, 128), F32)]
    return call(columns_kernel, (64, 8, 128), scratch, [params, field] + constants, scalars=1)


def image_from(field):
    constants = [jnp.asarray(c) for c in image_constants()]
    return call(image_kernel, (8, 16, 512), [], [field] + constants)


def exchange(field, axes):
    return lax.all_to_all(field, axes, split_axis=0, concat_axis=0, tiled=True)


def local(holograms, fresnel, ctf_terms):
    field = holograms.reshape(4, 8, 16, 512).transpose(1, 0, 2, 3)
    field = image_rows(exchange(field, "col"))
    field = filter_columns(exchange(field, ("row", "col")), fresnel, ctf_terms)
    field = exchange(field.reshape(256, 2, 128), ("row", "col"))
    image = image_from(field.reshape(512, 128))
    return exchange(image, "col").reshape(128, 512)


def solution(mesh):
    in_specs = (P(None, "row", "col"), P(), P())
    out_specs = P("row", "col")
    return jax.shard_map(local, mesh=mesh, in_specs=in_specs, out_specs=out_specs, check_vma=False)
```

```python
import math

import jax
import jax.numpy as jnp
import ml_dtypes
import numpy as np
from jax import lax
from jax.experimental import pallas as pl
from jax.experimental.pallas import tpu as pltpu
from jax.sharding import PartitionSpec as P

N = 4096
POS, NEG, ZERO, HALF = range(4)
F32 = jnp.float32
BF16 = jnp.bfloat16


def residues(quad):
    low, high = 2 * quad, 2 * quad + 1
    if quad == 0:
        return [0, 1, 16, 31]
    return [low, high, 32 - low, 32 - high]


def member(kind, group, slot):
    if kind == POS:
        return 4 * group + slot
    if kind == NEG:
        return 127 - 4 * group - slot
    if kind == ZERO:
        return [2 * group, 2 * group + 1, 128 - 2 * group if group else 64, 127 - 2 * group][slot]
    return [2 * group, 2 * group + 1, 127 - 2 * group, 126 - 2 * group][slot]


def halves(matrix):
    high = matrix.astype(ml_dtypes.bfloat16)
    low = (matrix - high.astype(np.float64)).astype(ml_dtypes.bfloat16)
    return np.stack([high, low])


def turn(product, length):
    angle = 2.0 * np.pi * (np.asarray(product, np.int64) % length) / length
    return np.cos(angle), np.sin(angle)


def row_constants():
    mats = []
    for kind in range(4):
        k2 = np.array([[member(kind, g, s) for s in range(4)] for g in range(32)])
        cosine, sine = turn(k2[:, :, None] * np.arange(128), 128)
        real = np.concatenate([cosine, sine], -1)
        imag = np.concatenate([-sine, cosine], -1)
        both = np.stack([real.reshape(32, 2, 2, 256), imag.reshape(32, 2, 2, 256)], 2)
        mats.append(halves(both.reshape(256, 256)))
    twist = np.stack(turn(np.arange(32)[:, None] * np.arange(128), N)).astype(np.float32)
    return np.stack(mats), twist


def column_constants():
    cosine, sine = turn(np.arange(16)[:, None] * np.arange(16), 16)
    eye8 = np.eye(8)
    forward = np.block(
        [
            [np.kron(eye8, cosine), np.kron(eye8, -sine)],
            [np.kron(eye8, sine), np.kron(eye8, cosine)],
        ]
    )
    pick = np.kron(np.eye(4), np.ones((2, 1)))
    twice = np.ones((1, 2))

    def spread(block):
        return np.kron(twice, np.kron(pick, block))

    inverse = np.block([[spread(cosine), spread(sine)], [spread(-sine), spread(cosine)]])
    lane = np.arange(128)
    within = lane % 16
    top = lane // 64
    step = np.arange(128)[None, :, None] + 128 * np.arange(2)[:, None, None]
    ahead = np.stack(turn(step * within, N)).astype(np.float32)
    step = np.arange(64)[None, :, None] + 128 * np.arange(2)[:, None, None] + 64 * top
    behind = np.stack(turn(step * within, N)).astype(np.float32)
    step = np.arange(2)[:, None, None] + 2 * top
    spin = np.stack(turn(step * np.arange(64)[None, :, None], 256)).astype(np.float32)
    return np.concatenate([halves(forward), halves(inverse)]), ahead, np.stack([behind, spin])


def image_constants():
    mats = []
    for kind in range(4):
        k2 = np.array([[member(kind, g, s) for g in range(32)] for s in range(4)])
        k2 = k2.reshape(2, 2, 32).transpose(0, 2, 1).reshape(2, 64)
        cosine, sine = turn(np.arange(128)[:, None, None] * k2, 128)
        real = np.stack([cosine, -sine], 2).reshape(128, 256)
        imag = np.stack([sine, cosine], 2).reshape(128, 256)
        mats.append(halves(np.concatenate([real, imag])))
    lane = np.arange(256)
    quad = 4 * (lane // 128) + 2 * (lane // 64 % 2) + lane // 8 % 2
    k1 = np.array([residues(q)[s] for q, s in zip(quad, lane // 16 % 4)])
    twist = np.stack(turn(np.arange(128)[:, None] * k1, N)).astype(np.float32)
    cosine, sine = turn(np.arange(32)[:, None] * k1, 32)
    same = (np.arange(8)[:, None] == lane % 8).astype(np.float64)
    real = np.concatenate([cosine[:, None] * same, -sine[:, None] * same], -1)
    imag = np.concatenate([sine[:, None] * same, cosine[:, None] * same], -1)
    last = np.concatenate([real, imag], 1).reshape(512, 512) * (0.5 / (N * N))
    return np.stack(mats), twist, halves(last)


def turned(value, angle_index, length, sign):
    angle_index %= length
    real, imag = value
    if angle_index == 0:
        return value
    if 4 * angle_index == length:
        return (-imag, real) if sign > 0 else (imag, -real)
    if 2 * angle_index == length:
        return (-real, -imag)
    if 4 * angle_index == 3 * length:
        return (imag, -real) if sign > 0 else (-imag, real)
    angle = sign * 2.0 * math.pi * angle_index / length
    cosine, sine = math.cos(angle), math.sin(angle)
    if (8 * angle_index) % length == 0:
        scale = abs(cosine)
        plus, minus = (real + imag) * scale, (real - imag) * scale
        if cosine > 0:
            return (minus, plus) if sine > 0 else (plus, -minus)
        return (-plus, minus) if sine > 0 else (-minus, -plus)
    return (real * cosine - imag * sine, imag * cosine + real * sine)


def plus(a, b):
    return (a[0] + b[0], a[1] + b[1])


def minus(a, b):
    return (a[0] - b[0], a[1] - b[1])


def transform(values, sign):
    length = len(values)
    if length == 1:
        return values
    if length == 2:
        return [plus(values[0], values[1]), minus(values[0], values[1])]
    quarter = length // 4
    columns = []
    for b in range(quarter):
        z0, z1, z2, z3 = (values[a * quarter + b] for a in range(4))
        even, odd = plus(z0, z2), plus(z1, z3)
        even_gap, odd_gap = minus(z0, z2), turned(minus(z1, z3), 1, 4, sign)
        outs = [plus(even, odd), plus(even_gap, odd_gap), minus(even, odd), minus(even_gap, odd_gap)]
        columns.append([turned(z, b * k, length, sign) for k, z in enumerate(outs)])
    result = [None] * length
    for k in range(4):
        for m, z in enumerate(transform([columns[b][k] for b in range(quarter)], sign)):
            result[k + 4 * m] = z
    return result


def times(value, cosine, sine):
    real, imag = value
    return (real * cosine - imag * sine, imag * cosine + real * sine)


def split(value):
    high = value.astype(BF16)
    return high, (value - high.astype(F32)).astype(BF16)


def product(left, right, dims):
    def one(a, b):
        return lax.dot_general(a, b, (dims, ((), ())), preferred_element_type=F32)

    return one(left[0], right[0]) + (one(left[0], right[1]) + one(left[1], right[0]))


def rows_kernel(field_ref, mats_ref, twist_ref, out_ref, high_ref, low_ref):
    for j in range(2):
        lines = []
        for n1 in range(32):
            at = pl.ds(128 * (n1 % 4), 128)
            lines.append(
                (field_ref[n1 // 4, 2 * j, :, at], field_ref[n1 // 4, 2 * j + 1, :, at])
            )
        lines = transform(lines, -1)
        for quad in range(8):
            for slot, k1 in enumerate(residues(quad)):
                line = lines[k1]
                if k1:
                    line = times(line, twist_ref[0, pl.ds(k1, 1), :], -twist_ref[1, pl.ds(k1, 1), :])
                rows = pl.ds(128 * quad + 32 * slot + 16 * j, 16)
                for part in range(2):
                    high, low = split(line[part])
                    high_ref[rows, pl.ds(128 * part, 128)] = high
                    low_ref[rows, pl.ds(128 * part, 128)] = low
    lane = lax.broadcasted_iota(jnp.int32, (256, 128), 1)
    for pair in range(4):
        rows = pl.ds(256 * pair, 256)
        data = (high_ref[rows, :], low_ref[rows, :])

        def mixed(kind):
            return product((mats_ref[kind, 0], mats_ref[kind, 1]), data, ((1,), (1,)))

        low_half, high_half = mixed(POS), mixed(NEG)
        if pair == 0:
            zero, half = mixed(ZERO), mixed(HALF)
        for side in range(2):
            at = slice(128 * side, 128 * side + 128)
            block = jnp.where(lane < 64, low_half[:, at], high_half[:, at])
            if pair == 0 and side == 0:
                block = jnp.where(lane < 32, zero[:, at], block)
                block = jnp.where((lane >= 64) & (lane < 96), half[:, at], block)
            out_ref[pl.ds(64 * pair + 32 * side, 32)] = block.reshape(32, 8, 128)


def sine_turns(turns):
    t = turns - jnp.round(turns)
    square = t * t
    total = SINE[-1]
    for coefficient in SINE[-2::-1]:
        total = total * square + coefficient
    return total * t


def sine_fit():
    nodes = np.cos(np.pi * (np.arange(400) + 0.5) / 800) * 0.5
    basis = np.stack([nodes ** (2 * k + 1) for k in range(8)], 1)
    return [float(c) for c in np.linalg.lstsq(basis, np.sin(2 * np.pi * nodes), rcond=None)[0]]


SINE = sine_fit()


def device_number():
    return 8 * lax.axis_index("row") + lax.axis_index("col")


def arc_tangent(value):
    for _ in range(2):
        value = value / (1.0 + jnp.sqrt(1.0 + value * value))
    square = value * value
    total = 1.0 / 17.0
    for k in range(15, 0, -2):
        total = 1.0 / k - square * total
    return 4.0 * value * total


def columns_kernel(
    fresnel_ref,
    terms_ref,
    field_ref,
    mats_hbm,
    ahead_hbm,
    behind_hbm,
    out_ref,
    work_ref,
    back_ref,
    mats_ref,
    ahead_ref,
    behind_ref,
    sems,
):
    copies = [
        pltpu.make_async_copy(source, target, sems.at[k])
        for k, (source, target) in enumerate(
            [(mats_hbm, mats_ref), (ahead_hbm, ahead_ref), (behind_hbm, behind_ref)]
        )
    ]
    for copy in copies:
        copy.start()
    device = device_number()
    quad, group = device // 32, device % 32
    sub = lax.broadcasted_iota(jnp.int32, (8, 128), 0)
    lane = lax.broadcasted_iota(jnp.int32, (8, 128), 1)
    first = (sub & 2) == 0
    sign = jnp.where(first, 1.0, -1.0).astype(F32)
    side = jnp.where(lane < 64, 1.0, -1.0).astype(F32)

    def shift(value, amount, axis):
        return pltpu.roll(value, amount, axis + value.ndim - 2)

    def swap_pairs(value):
        return jnp.where(first, shift(value, 6, 0), shift(value, 2, 0))

    for nb in range(8):
        lines = []
        for na in range(16):
            n = 8 * na + nb
            one, two = field_ref[2 * n], field_ref[2 * n + 1]
            lines.append(
                (jnp.where(first, one, shift(two, 2, 0)), jnp.where(first, shift(one, 6, 0), two))
            )
        for ka, line in enumerate(transform(lines, -1)):
            real, imag = turned(line, nb * ka, 128, -1)
            work_ref[0, ka, nb] = real
            work_ref[1, ka, nb] = imag

    slot = lane >> 5
    s = ((sub >> 2) << 1) | (sub & 1)
    positive = 4 * group + s
    base = 2 * group + (s & 1)
    mirrored = jnp.where(s < 2, base, jnp.where(base == 0, 64, 128 - base))
    halfway = jnp.where(s < 2, base, 127 - base)
    k2 = jnp.where(slot < 2, positive, 127 - positive)
    k1 = 2 * quad + (slot & 1)
    k1 = jnp.where(slot < 2, k1, 32 - k1)
    special = (quad == 0) & ((slot & 1) == 0)
    k2 = jnp.where(special, jnp.where(slot == 0, mirrored, halfway), k2)
    k1 = jnp.where(special, jnp.where(slot == 0, 0, 16), k1)
    v = k1 + 32 * k2
    v = jnp.where(v >= N // 2, v - N, v).astype(F32)
    v_square = v * v
    a2 = lane & 15
    u_base = (64 * (sub & 2) + 256 * a2 - jnp.where(a2 >= 8, N, 0)).astype(F32)
    later = (lane & 16) != 0
    rate_even = (0.5 / (N * N)) / jnp.where(later, fresnel_ref[2], fresnel_ref[0])
    rate_odd = (0.5 / (N * N)) / jnp.where(later, fresnel_ref[3], fresnel_ref[1])
    ratio = jnp.full((8, 128), terms_ref[0], F32)
    offset = arc_tangent(ratio) * (0.5 / math.pi)
    gain = 2.0 * jnp.sqrt(1.0 + ratio * ratio)
    floor = terms_ref[1]

    def rows_of(table, which, start, count, stride):
        picked = []
        for part in range(2):
            tiles = []
            for k in range(count):
                at = pl.ds(start + stride * k, 1)
                upper = jnp.broadcast_to(table[which + (part, 0, at)], (8, 128))
                lower = jnp.broadcast_to(table[which + (part, 1, at)], (8, 128))
                tiles.append(jnp.where(first, upper, lower))
            picked.append(jnp.stack(tiles))
        return picked

    for copy in copies:
        copy.wait()
    forward = (mats_ref[0], mats_ref[1])
    inverse = (mats_ref[2], mats_ref[3])
    natural = ((1,), (0,))
    for bunch in range(4):
        reals, imags = [], []
        for ka in range(4 * bunch, 4 * bunch + 4):
            lines = transform([(work_ref[0, ka, nb], work_ref[1, ka, nb]) for nb in range(8)], -1)
            turned_lines = []
            for kb, line in enumerate(lines):
                angle = 2.0 * math.pi * (ka + 16 * kb) / 256
                line = times(
                    line,
                    jnp.where(first, 1.0, math.cos(angle)).astype(F32),
                    jnp.where(first, 0.0, -math.sin(angle)).astype(F32),
                )
                turned_lines.append(tuple(swap_pairs(z) + sign * z for z in line))
            real = jnp.stack([z[0] for z in turned_lines])
            imag = jnp.stack([z[1] for z in turned_lines])
            cosine, sine = rows_of(ahead_ref, (), ka, 8, 16)
            real, imag = times((real, imag), cosine, -sine)
            reals.append(real.reshape(64, 128))
            imags.append(imag.reshape(64, 128))
        mixed = jnp.concatenate(
            [jnp.concatenate(reals, 0), jnp.concatenate(imags, 0)], 1
        )
        mixed = product(split(mixed), forward, natural)
        reals, imags = [], []
        for step in range(4):
            ka = 4 * bunch + step
            rows = slice(64 * step, 64 * step + 64)
            real = mixed[rows, :128].reshape(8, 8, 128)
            imag = mixed[rows, 128:].reshape(8, 8, 128)
            w1 = ka + 16 * lax.broadcasted_iota(jnp.int32, (8, 8, 128), 0)
            u = u_base + w1.astype(F32)
            radius = u * u + v_square
            even = gain * sine_turns(radius * rate_even + offset)
            odd = gain * sine_turns(radius * rate_odd + offset)
            energy = even * even + odd * odd
            other = jnp.where(later, shift(energy, 16, 1), shift(energy, 112, 1))
            scale = 1.0 / (energy + other + floor)
            reals.append(((even * real + odd * imag) * scale).reshape(64, 128))
            imags.append(((even * imag - odd * real) * scale).reshape(64, 128))
        mixed = jnp.concatenate(
            [jnp.concatenate(reals, 0), jnp.concatenate(imags, 0)], 1
        )
        mixed = product(split(mixed), inverse, natural)
        for step in range(4):
            ka = 4 * bunch + step
            rows = slice(64 * step, 64 * step + 64)
            real = mixed[rows, :128].reshape(8, 8, 128)
            imag = mixed[rows, 128:].reshape(8, 8, 128)
            real = jnp.where(lane < 64, real[:4], real[4:])
            imag = jnp.where(lane < 64, imag[:4], imag[4:])
            cosine, sine = rows_of(behind_ref, (0,), ka, 4, 16)
            real, imag = times((real, imag), cosine, sine)
            real, imag = (swap_pairs(z) + sign * z for z in (real, imag))
            corner = (lane >= 64) & jnp.logical_not(first)
            real, imag = jnp.where(corner, -imag, real), jnp.where(corner, real, imag)
            real, imag = (shift(z, 64, 1) + side * z for z in (real, imag))
            cosine, sine = rows_of(behind_ref, (1,), ka, 4, 16)
            real, imag = times((real, imag), cosine, sine)
            back_ref[0, ka] = real
            back_ref[1, ka] = imag

    for wb in range(8):
        lines = [
            tuple(back_ref[part, wb + 8 * (wa % 2), wa // 2] for part in range(2)) for wa in range(8)
        ]
        for na, line in enumerate(transform(lines, 1)):
            real, imag = turned(line, wb * na, 64, 1)
            work_ref[0, na, wb] = real
            work_ref[1, na, wb] = imag
    bit5 = (lane & 32) != 0
    reflected = (quad == 0) & ((lane & 16) == 0)
    itself = (quad == 0) & (group == 0) & ((lane & 48) == 0) & ((sub & 1) == 0)
    low_half = (lane & 8) == 0
    straight = ((sub & 4) != 0) == (lane >= 64)

    def partner(value):
        across = jnp.where(bit5, shift(value, 32, 1), shift(value, 96, 1))
        down = jnp.where(itself, value, shift(value, 4, 0))
        return jnp.where(reflected, down, across)

    for na in range(8):
        lines = [(work_ref[0, na, wb], work_ref[1, na, wb]) for wb in range(8)]
        for nb, (real, imag) in enumerate(transform(lines, 1)):
            real, imag = real + partner(real), imag - partner(imag)
            packed = real + jnp.where(low_half, -shift(imag, 120, 1), shift(imag, 8, 1))
            crossed = shift(shift(packed, 64, 1), 4, 0)
            out_ref[na + 8 * nb] = jnp.where(straight, packed, crossed)


def image_kernel(field_ref, mats_ref, twist_ref, last_ref, out_ref):
    lane = lax.broadcasted_iota(jnp.int32, (64, 128), 1)
    bit6, bit3 = (lane & 64) != 0, (lane & 8) != 0
    blocks = []
    for pair in range(2):
        tiles = [field_ref[pl.ds(256 * pair + 64 * q, 64), :] for q in range(4)]
        parts = []
        for qb in range(2):
            one, two = tiles[qb], tiles[2 + qb]
            parts.append(
                (
                    jnp.where(bit6, pltpu.roll(two, 64, 1), one),
                    jnp.where(bit6, two, pltpu.roll(one, 64, 1)),
                )
            )
        stacked = []
        for s1 in range(2):
            one, two = parts[0][s1], parts[1][s1]
            stacked.append(jnp.where(bit3, pltpu.roll(two, 8, 1), one))
            stacked.append(jnp.where(bit3, two, pltpu.roll(one, 120, 1)))
        blocks.append(jnp.concatenate(stacked, 0))
    data = split(jnp.concatenate(blocks, 1))

    def mixed(kind):
        return product((mats_ref[kind, 0], mats_ref[kind, 1]), data, ((1,), (0,)))

    lane = lax.broadcasted_iota(jnp.int32, (256, 256), 1)
    value = jnp.where((lane & 32) == 0, mixed(POS), mixed(NEG))
    value = jnp.where((lane & (128 + 64 + 32 + 16 + 8)) == 0, mixed(ZERO), value)
    value = jnp.where((lane & (128 + 64 + 32 + 16 + 8)) == 32, mixed(HALF), value)
    real, imag = times((value[:128], value[128:]), twist_ref[0], twist_ref[1])
    lines = split(jnp.concatenate([real, imag], 1))
    image = product((last_ref[0], last_ref[1]), lines, ((1,), (1,)))
    for n1 in range(32):
        out_ref[n1 // 4, :, pl.ds(128 * (n1 % 4), 128)] = image[16 * n1 : 16 * n1 + 16]


def call(kernel, out_shape, scratch, arguments, spaces):
    return pl.pallas_call(
        kernel,
        out_shape=jax.ShapeDtypeStruct(out_shape, F32),
        in_specs=[pl.BlockSpec(memory_space=space) for space in spaces],
        out_specs=pl.BlockSpec(memory_space=pltpu.VMEM),
        scratch_shapes=scratch,
        compiler_params=pltpu.CompilerParams(vmem_limit_bytes=40 * 1024 * 1024),
    )(*arguments)


def image_rows(field):
    arguments = [field] + [jnp.asarray(c) for c in row_constants()]
    scratch = [pltpu.VMEM((1024, 256), BF16), pltpu.VMEM((1024, 256), BF16)]
    return call(rows_kernel, (256, 8, 128), scratch, arguments, [pltpu.VMEM] * 3)


def filter_columns(field, fresnel, ctf_terms):
    constants = [jnp.asarray(c) for c in column_constants()]
    scratch = [pltpu.VMEM((2, 16, 8, 8, 128), F32), pltpu.VMEM((2, 16, 4, 8, 128), F32)]
    scratch += [pltpu.VMEM(c.shape, c.dtype) for c in constants] + [pltpu.SemaphoreType.DMA((3,))]
    spaces = [pltpu.SMEM] * 2 + [pltpu.VMEM] + [pltpu.HBM] * 3
    arguments = [fresnel, ctf_terms, field] + constants
    return call(columns_kernel, (64, 8, 128), scratch, arguments, spaces)


def image_from(field):
    arguments = [field] + [jnp.asarray(c) for c in image_constants()]
    return call(image_kernel, (8, 16, 512), [], arguments, [pltpu.VMEM] * 4)


def exchange(field, axes):
    return lax.all_to_all(field, axes, split_axis=0, concat_axis=0, tiled=True)


def local(holograms, fresnel, ctf_terms):
    field = holograms.reshape(4, 8, 16, 512).transpose(1, 0, 2, 3)
    field = image_rows(exchange(field, "col"))
    field = filter_columns(exchange(field, ("row", "col")), fresnel, ctf_terms)
    field = exchange(field.reshape(256, 2, 128), ("row", "col"))
    image = image_from(field.reshape(512, 128))
    return exchange(image, "col").reshape(128, 512)


def solution(mesh):
    in_specs = (P(None, "row", "col"), P(), P())
    out_specs = P("row", "col")
    return jax.shard_map(local, mesh=mesh, in_specs=in_specs, out_specs=out_specs, check_vma=False)
```

```python
import math

import jax
import jax.numpy as jnp
import ml_dtypes
import numpy as np
from jax import lax
from jax.experimental import pallas as pl
from jax.experimental.pallas import tpu as pltpu
from jax.sharding import PartitionSpec as P

N = 4096
POS, NEG, ZERO, HALF = range(4)
F32 = jnp.float32
BF16 = jnp.bfloat16


def residues(quad):
    low, high = 2 * quad, 2 * quad + 1
    if quad == 0:
        return [0, 1, 16, 31]
    if quad % 2:
        return [32 - low, 32 - high, low, high]
    return [low, high, 32 - low, 32 - high]


def member(kind, group, slot):
    if kind == POS:
        return 4 * group + slot
    if kind == NEG:
        return 127 - 4 * group - slot
    if kind == ZERO:
        return [2 * group, 2 * group + 1, 128 - 2 * group if group else 64, 127 - 2 * group][slot]
    return [2 * group, 2 * group + 1, 127 - 2 * group, 126 - 2 * group][slot]


def halves(matrix):
    high = matrix.astype(ml_dtypes.bfloat16)
    low = (matrix - high.astype(np.float64)).astype(ml_dtypes.bfloat16)
    return np.stack([high, low])


def turn(product, length):
    angle = 2.0 * np.pi * (np.asarray(product, np.int64) % length) / length
    return np.cos(angle), np.sin(angle)


def line_twist():
    return np.stack(turn(np.arange(32)[:, None] * np.arange(128), N)).astype(np.float32)


def row_constants():
    mats = []
    for kind in range(4):
        k2 = np.array([[member(kind, g, s) for s in range(4)] for g in range(32)])
        cosine, sine = turn(k2[:, :, None] * np.arange(128), 128)
        real = np.concatenate([cosine, sine], -1)
        imag = np.concatenate([-sine, cosine], -1)
        both = np.stack([real.reshape(32, 2, 2, 256), imag.reshape(32, 2, 2, 256)], 2)
        mats.append(halves(both.reshape(256, 256)))
    return np.stack(mats), line_twist()


def column_constants():
    cosine, sine = turn(np.arange(16)[:, None] * np.arange(16), 16)
    eye8 = np.eye(8)
    forward = np.block(
        [
            [np.kron(eye8, cosine), np.kron(eye8, -sine)],
            [np.kron(eye8, sine), np.kron(eye8, cosine)],
        ]
    )
    pick = np.kron(np.eye(4), np.ones((2, 1)))
    twice = np.ones((1, 2))

    def spread(block):
        return np.kron(twice, np.kron(pick, block))

    inverse = np.block([[spread(cosine), spread(sine)], [spread(-sine), spread(cosine)]])
    lane = np.arange(128)
    within = lane % 16
    top = lane // 64
    step = np.arange(128)[None, :, None] + 128 * np.arange(2)[:, None, None]
    ahead = np.stack(turn(step * within, N)).astype(np.float32)
    step = np.arange(64)[None, :, None] + 128 * np.arange(2)[:, None, None] + 64 * top
    behind = np.stack(turn(step * within, N)).astype(np.float32)
    step = np.arange(2)[:, None, None] + 2 * top
    spin = np.stack(turn(step * np.arange(64)[None, :, None], 256)).astype(np.float32)
    return np.concatenate([halves(forward), halves(inverse)]), ahead, np.stack([behind, spin])


def image_constants():
    mats = []
    for kind in range(4):
        k2 = np.array([[member(kind, g, s) for g in range(32)] for s in range(4)])
        k2 = k2.reshape(2, 2, 32).transpose(0, 2, 1).reshape(2, 64)
        cosine, sine = turn(k2[:, :, None] * np.arange(128), 128)
        real = np.concatenate([cosine, sine], -1)
        imag = np.concatenate([-sine, cosine], -1)
        mats.append(halves(np.stack([real, imag], 1).reshape(256, 256) * (0.5 / (N * N))))
    return np.stack(mats), line_twist()


def turned(value, angle_index, length, sign):
    angle_index %= length
    real, imag = value
    if angle_index == 0:
        return value
    if 4 * angle_index == length:
        return (-imag, real) if sign > 0 else (imag, -real)
    if 2 * angle_index == length:
        return (-real, -imag)
    if 4 * angle_index == 3 * length:
        return (imag, -real) if sign > 0 else (-imag, real)
    angle = sign * 2.0 * math.pi * angle_index / length
    cosine, sine = math.cos(angle), math.sin(angle)
    if (8 * angle_index) % length == 0:
        scale = abs(cosine)
        plus, minus = (real + imag) * scale, (real - imag) * scale
        if cosine > 0:
            return (minus, plus) if sine > 0 else (plus, -minus)
        return (-plus, minus) if sine > 0 else (-minus, -plus)
    return (real * cosine - imag * sine, imag * cosine + real * sine)


def plus(a, b):
    return (a[0] + b[0], a[1] + b[1])


def minus(a, b):
    return (a[0] - b[0], a[1] - b[1])


def transform(values, sign):
    length = len(values)
    if length == 1:
        return values
    if length == 2:
        return [plus(values[0], values[1]), minus(values[0], values[1])]
    quarter = length // 4
    columns = []
    for b in range(quarter):
        z0, z1, z2, z3 = (values[a * quarter + b] for a in range(4))
        even, odd = plus(z0, z2), plus(z1, z3)
        even_gap, odd_gap = minus(z0, z2), turned(minus(z1, z3), 1, 4, sign)
        outs = [plus(even, odd), plus(even_gap, odd_gap), minus(even, odd), minus(even_gap, odd_gap)]
        columns.append([turned(z, b * k, length, sign) for k, z in enumerate(outs)])
    result = [None] * length
    for k in range(4):
        for m, z in enumerate(transform([columns[b][k] for b in range(quarter)], sign)):
            result[k + 4 * m] = z
    return result


def times(value, cosine, sine):
    real, imag = value
    return (real * cosine - imag * sine, imag * cosine + real * sine)


def split(value):
    high = value.astype(BF16)
    return high, (value - high.astype(F32)).astype(BF16)


def product(left, right, dims):
    def one(a, b):
        return lax.dot_general(a, b, (dims, ((), ())), preferred_element_type=F32)

    return one(left[0], right[0]) + (one(left[0], right[1]) + one(left[1], right[0]))


def rows_kernel(field_ref, mats_ref, twist_ref, out_ref, high_ref, low_ref):
    for j in range(2):
        lines = []
        for n1 in range(32):
            at = pl.ds(128 * (n1 % 4), 128)
            lines.append(
                (field_ref[n1 // 4, 2 * j, :, at], field_ref[n1 // 4, 2 * j + 1, :, at])
            )
        lines = transform(lines, -1)
        for k1, line in enumerate(lines):
            if k1:
                line = times(line, twist_ref[0, pl.ds(k1, 1), :], -twist_ref[1, pl.ds(k1, 1), :])
            place = 32 * k1 if k1 < 16 else 512 + 32 * ((32 - k1) % 16 ^ 2)
            rows = pl.ds(place + 16 * j, 16)
            for part in range(2):
                high, low = split(line[part])
                high_ref[rows, pl.ds(128 * part, 128)] = high
                low_ref[rows, pl.ds(128 * part, 128)] = low

    def mixed(kind, start, count):
        rows = pl.ds(start, count)
        data = (high_ref[rows, :], low_ref[rows, :])
        return product((mats_ref[kind, 0], mats_ref[kind, 1]), data, ((1,), (1,)))

    lane = lax.broadcasted_iota(jnp.int32, (256, 128), 1)
    for half in range(2):
        positive, negative = mixed(POS, 256 * half, 256), mixed(NEG, 512 + 256 * half, 256)
        for pair in range(2):
            at = slice(128 * pair, 128 * pair + 128)
            one, two = positive[:, at], negative[:, at]
            even, odd = jnp.where(lane < 64, one, two), jnp.where(lane < 64, two, one)
            if half == 0 and pair == 0:
                even = jnp.where(lane < 32, mixed(ZERO, 0, 128), even)
                even = jnp.where((lane & 96) == 64, mixed(HALF, 512, 128), even)
            for side, block in enumerate([even, odd]):
                quad = 4 * half + 2 * pair + side
                out_ref[pl.ds(32 * quad, 32)] = block.reshape(32, 8, 128)


def sine_turns(turns):
    t = turns - jnp.round(turns)
    square = t * t
    total = SINE[-1]
    for coefficient in SINE[-2::-1]:
        total = total * square + coefficient
    return total * t


def sine_fit():
    nodes = np.cos(np.pi * (np.arange(400) + 0.5) / 800) * 0.5
    basis = np.stack([nodes ** (2 * k + 1) for k in range(6)], 1)
    return [float(c) for c in np.linalg.lstsq(basis, np.sin(2 * np.pi * nodes), rcond=None)[0]]


SINE = sine_fit()


def device_number():
    return 8 * lax.axis_index("row") + lax.axis_index("col")


def arc_tangent(value):
    for _ in range(2):
        value = value / (1.0 + jnp.sqrt(1.0 + value * value))
    square = value * value
    total = 1.0 / 17.0
    for k in range(15, 0, -2):
        total = 1.0 / k - square * total
    return 4.0 * value * total


def columns_kernel(
    fresnel_ref,
    terms_ref,
    field_ref,
    mats_hbm,
    ahead_hbm,
    behind_hbm,
    out_ref,
    work_ref,
    back_ref,
    mats_ref,
    ahead_ref,
    behind_ref,
    sems,
):
    copies = [
        pltpu.make_async_copy(source, target, sems.at[k])
        for k, (source, target) in enumerate(
            [(mats_hbm, mats_ref), (ahead_hbm, ahead_ref), (behind_hbm, behind_ref)]
        )
    ]
    for copy in copies:
        copy.start()
    device = device_number()
    quad, group = device // 32, device % 32
    sub = lax.broadcasted_iota(jnp.int32, (8, 128), 0)
    lane = lax.broadcasted_iota(jnp.int32, (8, 128), 1)
    first = (sub & 2) == 0
    sign = jnp.where(first, 1.0, -1.0).astype(F32)
    side = jnp.where(lane < 64, 1.0, -1.0).astype(F32)

    def shift(value, amount, axis):
        return pltpu.roll(value, amount, axis + value.ndim - 2)

    def swap_pairs(value):
        return jnp.where(first, shift(value, 6, 0), shift(value, 2, 0))

    for nb in range(8):
        lines = []
        for na in range(16):
            n = 8 * na + nb
            one, two = field_ref[2 * n], field_ref[2 * n + 1]
            lines.append(
                (jnp.where(first, one, shift(two, 2, 0)), jnp.where(first, shift(one, 6, 0), two))
            )
        for ka, line in enumerate(transform(lines, -1)):
            real, imag = turned(line, nb * ka, 128, -1)
            work_ref[0, ka, nb] = real
            work_ref[1, ka, nb] = imag

    slot = (lane >> 5) ^ (2 * (quad & 1))
    s = ((sub >> 2) << 1) | (sub & 1)
    positive = 4 * group + s
    base = 2 * group + (s & 1)
    mirrored = jnp.where(s < 2, base, jnp.where(base == 0, 64, 128 - base))
    halfway = jnp.where(s < 2, base, 127 - base)
    k2 = jnp.where(slot < 2, positive, 127 - positive)
    k1 = 2 * quad + (slot & 1)
    k1 = jnp.where(slot < 2, k1, 32 - k1)
    special = (quad == 0) & ((slot & 1) == 0)
    k2 = jnp.where(special, jnp.where(slot == 0, mirrored, halfway), k2)
    k1 = jnp.where(special, jnp.where(slot == 0, 0, 16), k1)
    v = k1 + 32 * k2
    v = jnp.where(v >= N // 2, v - N, v).astype(F32)
    v_square = v * v
    a2 = lane & 15
    u_base = (64 * (sub & 2) + 256 * a2 - jnp.where(a2 >= 8, N, 0)).astype(F32)
    later = (lane & 16) != 0
    rate_even = (0.5 / (N * N)) / jnp.where(later, fresnel_ref[2], fresnel_ref[0])
    rate_odd = (0.5 / (N * N)) / jnp.where(later, fresnel_ref[3], fresnel_ref[1])
    ratio = jnp.full((8, 128), terms_ref[0], F32)
    offset = arc_tangent(ratio) * (0.5 / math.pi)
    gain = 2.0 * jnp.sqrt(1.0 + ratio * ratio)
    floor = terms_ref[1]

    def rows_of(table, which, start, count, stride):
        picked = []
        for part in range(2):
            tiles = []
            for k in range(count):
                at = pl.ds(start + stride * k, 1)
                upper = jnp.broadcast_to(table[which + (part, 0, at)], (8, 128))
                lower = jnp.broadcast_to(table[which + (part, 1, at)], (8, 128))
                tiles.append(jnp.where(first, upper, lower))
            picked.append(jnp.stack(tiles))
        return picked

    for copy in copies:
        copy.wait()
    forward = (mats_ref[0], mats_ref[1])
    inverse = (mats_ref[2], mats_ref[3])
    natural = ((1,), (0,))
    for bunch in range(4):
        reals, imags = [], []
        for ka in range(4 * bunch, 4 * bunch + 4):
            lines = transform([(work_ref[0, ka, nb], work_ref[1, ka, nb]) for nb in range(8)], -1)
            turned_lines = []
            for kb, line in enumerate(lines):
                angle = 2.0 * math.pi * (ka + 16 * kb) / 256
                line = times(
                    line,
                    jnp.where(first, 1.0, math.cos(angle)).astype(F32),
                    jnp.where(first, 0.0, -math.sin(angle)).astype(F32),
                )
                turned_lines.append(tuple(swap_pairs(z) + sign * z for z in line))
            real = jnp.stack([z[0] for z in turned_lines])
            imag = jnp.stack([z[1] for z in turned_lines])
            cosine, sine = rows_of(ahead_ref, (), ka, 8, 16)
            real, imag = times((real, imag), cosine, -sine)
            reals.append(real.reshape(64, 128))
            imags.append(imag.reshape(64, 128))
        mixed = jnp.concatenate(
            [jnp.concatenate(reals, 0), jnp.concatenate(imags, 0)], 1
        )
        mixed = product(split(mixed), forward, natural)
        reals, imags = [], []
        for step in range(4):
            ka = 4 * bunch + step
            rows = slice(64 * step, 64 * step + 64)
            real = mixed[rows, :128].reshape(8, 8, 128)
            imag = mixed[rows, 128:].reshape(8, 8, 128)
            w1 = ka + 16 * lax.broadcasted_iota(jnp.int32, (8, 8, 128), 0)
            u = u_base + w1.astype(F32)
            radius = u * u + v_square
            even = gain * sine_turns(radius * rate_even + offset)
            odd = gain * sine_turns(radius * rate_odd + offset)
            energy = even * even + odd * odd
            other = jnp.where(later, shift(energy, 16, 1), shift(energy, 112, 1))
            scale = 1.0 / (energy + other + floor)
            reals.append(((even * real + odd * imag) * scale).reshape(64, 128))
            imags.append(((even * imag - odd * real) * scale).reshape(64, 128))
        mixed = jnp.concatenate(
            [jnp.concatenate(reals, 0), jnp.concatenate(imags, 0)], 1
        )
        mixed = product(split(mixed), inverse, natural)
        for step in range(4):
            ka = 4 * bunch + step
            rows = slice(64 * step, 64 * step + 64)
            real = mixed[rows, :128].reshape(8, 8, 128)
            imag = mixed[rows, 128:].reshape(8, 8, 128)
            real = jnp.where(lane < 64, real[:4], real[4:])
            imag = jnp.where(lane < 64, imag[:4], imag[4:])
            cosine, sine = rows_of(behind_ref, (0,), ka, 4, 16)
            real, imag = times((real, imag), cosine, sine)
            real, imag = (swap_pairs(z) + sign * z for z in (real, imag))
            corner = (lane >= 64) & jnp.logical_not(first)
            real, imag = jnp.where(corner, -imag, real), jnp.where(corner, real, imag)
            real, imag = (shift(z, 64, 1) + side * z for z in (real, imag))
            cosine, sine = rows_of(behind_ref, (1,), ka, 4, 16)
            real, imag = times((real, imag), cosine, sine)
            back_ref[0, ka] = real
            back_ref[1, ka] = imag

    for wb in range(8):
        lines = [
            tuple(back_ref[part, wb + 8 * (wa % 2), wa // 2] for part in range(2)) for wa in range(8)
        ]
        for na, line in enumerate(transform(lines, 1)):
            real, imag = turned(line, wb * na, 64, 1)
            work_ref[0, na, wb] = real
            work_ref[1, na, wb] = imag
    bit5 = (lane & 32) != 0
    reflected = (quad == 0) & ((lane & 16) == 0)
    itself = (quad == 0) & (group == 0) & ((lane & 48) == 0) & ((sub & 1) == 0)
    low_half = (lane & 8) == 0
    straight = ((sub & 4) != 0) == (lane >= 64)

    def partner(value):
        across = jnp.where(bit5, shift(value, 32, 1), shift(value, 96, 1))
        down = jnp.where(itself, value, shift(value, 4, 0))
        return jnp.where(reflected, down, across)

    for na in range(8):
        lines = [(work_ref[0, na, wb], work_ref[1, na, wb]) for wb in range(8)]
        for nb, (real, imag) in enumerate(transform(lines, 1)):
            real, imag = real + partner(real), imag - partner(imag)
            packed = real + jnp.where(low_half, -shift(imag, 120, 1), shift(imag, 8, 1))
            crossed = shift(shift(packed, 64, 1), 4, 0)
            out_ref[na + 8 * nb] = jnp.where(straight, packed, crossed)


def image_kernel(field_ref, mats_ref, twist_ref, out_ref):
    lane = lax.broadcasted_iota(jnp.int32, (64, 128), 1)
    bit6, bit3 = (lane & 64) != 0, (lane & 8) != 0
    tiles = {}
    for half in range(2):
        quads = [field_ref[pl.ds(256 * half + 64 * q, 64), :] for q in range(4)]
        parts = []
        for qb in range(2):
            one, two = quads[qb], quads[2 + qb]
            parts.append(
                (
                    jnp.where(bit6, pltpu.roll(two, 64, 1), one),
                    jnp.where(bit6, two, pltpu.roll(one, 64, 1)),
                )
            )
        stacked = []
        for s1 in range(2):
            one, two = parts[0][s1], parts[1][s1]
            stacked.append(jnp.where(bit3, pltpu.roll(two, 8, 1), one))
            stacked.append(jnp.where(bit3, two, pltpu.roll(one, 120, 1)))
        lines = jnp.concatenate(stacked, 0).T
        for q in range(4):
            for slot, k1 in enumerate(residues(4 * half + q)):
                start = 64 * (q // 2) + 16 * slot + 8 * (q % 2)
                tiles[k1] = lines[start : start + 8]
    lines = {}
    for kind, members in (
        (POS, [1, *range(1, 16)]),
        (NEG, [17, *range(17, 32)]),
        (ZERO, [0, 0]),
        (HALF, [16, 16]),
    ):
        data = split(jnp.concatenate([tiles[k1] for k1 in members], 0))
        value = product(data, (mats_ref[kind, 0], mats_ref[kind, 1]), ((1,), (0,)))
        for k, k1 in enumerate(members):
            line = (value[8 * k : 8 * k + 8, :128], value[8 * k : 8 * k + 8, 128:])
            lines[k1] = times(line, twist_ref[0, pl.ds(k1, 1), :], twist_ref[1, pl.ds(k1, 1), :])
    for n1, (real, imag) in enumerate(transform([lines[k1] for k1 in range(32)], 1)):
        at = pl.ds(128 * (n1 % 4), 128)
        out_ref[n1 // 4, pl.ds(0, 8), at] = real
        out_ref[n1 // 4, pl.ds(8, 8), at] = imag


def call(kernel, out_shape, scratch, arguments, spaces):
    return pl.pallas_call(
        kernel,
        out_shape=jax.ShapeDtypeStruct(out_shape, F32),
        in_specs=[pl.BlockSpec(memory_space=space) for space in spaces],
        out_specs=pl.BlockSpec(memory_space=pltpu.VMEM),
        scratch_shapes=scratch,
        compiler_params=pltpu.CompilerParams(vmem_limit_bytes=40 * 1024 * 1024),
    )(*arguments)


def image_rows(field):
    arguments = [field] + [jnp.asarray(c) for c in row_constants()]
    scratch = [pltpu.VMEM((1024, 256), BF16), pltpu.VMEM((1024, 256), BF16)]
    return call(rows_kernel, (256, 8, 128), scratch, arguments, [pltpu.VMEM] * 3)


def filter_columns(field, fresnel, ctf_terms):
    constants = [jnp.asarray(c) for c in column_constants()]
    scratch = [pltpu.VMEM((2, 16, 8, 8, 128), F32), pltpu.VMEM((2, 16, 4, 8, 128), F32)]
    scratch += [pltpu.VMEM(c.shape, c.dtype) for c in constants] + [pltpu.SemaphoreType.DMA((3,))]
    spaces = [pltpu.SMEM] * 2 + [pltpu.VMEM] + [pltpu.HBM] * 3
    arguments = [fresnel, ctf_terms, field] + constants
    return call(columns_kernel, (64, 8, 128), scratch, arguments, spaces)


def image_from(field):
    arguments = [field] + [jnp.asarray(c) for c in image_constants()]
    return call(image_kernel, (8, 16, 512), [], arguments, [pltpu.VMEM] * 3)


def exchange(field, axes):
    return lax.all_to_all(field, axes, split_axis=0, concat_axis=0, tiled=True)


def local(holograms, fresnel, ctf_terms):
    field = holograms.reshape(4, 8, 16, 512).transpose(1, 0, 2, 3)
    field = image_rows(exchange(field, "col"))
    field = filter_columns(exchange(field, ("row", "col")), fresnel, ctf_terms)
    field = exchange(field.reshape(256, 2, 128), ("row", "col"))
    image = image_from(field.reshape(512, 128))
    return exchange(image, "col").reshape(128, 512)


def solution(mesh):
    in_specs = (P(None, "row", "col"), P(), P())
    out_specs = P("row", "col")
    return jax.shard_map(local, mesh=mesh, in_specs=in_specs, out_specs=out_specs, check_vma=False)
```

```python
import math

import jax
import jax.numpy as jnp
import ml_dtypes
import numpy as np
from jax import lax
from jax.experimental import pallas as pl
from jax.experimental.pallas import tpu as pltpu
from jax.sharding import PartitionSpec as P

N = 4096
POS, NEG, ZERO, HALF = range(4)
ORDER = [128 * (place % 2) + place // 2 for place in range(256)]
F32 = jnp.float32
BF16 = jnp.bfloat16


def residues(quad):
    low, high = 2 * quad, 2 * quad + 1
    if quad == 0:
        return [0, 1, 16, 31]
    if quad % 2:
        return [32 - low, 32 - high, low, high]
    return [low, high, 32 - low, 32 - high]


def member(kind, group, slot):
    if kind == POS:
        return 4 * group + slot
    if kind == NEG:
        return 127 - 4 * group - slot
    if kind == ZERO:
        return [2 * group, 2 * group + 1, 128 - 2 * group if group else 64, 127 - 2 * group][slot]
    return [2 * group, 2 * group + 1, 127 - 2 * group, 126 - 2 * group][slot]


def halves(matrix):
    high = matrix.astype(ml_dtypes.bfloat16)
    low = (matrix - high.astype(np.float64)).astype(ml_dtypes.bfloat16)
    return np.stack([high, low])


def turn(product, length):
    angle = 2.0 * np.pi * (np.asarray(product, np.int64) % length) / length
    return np.cos(angle), np.sin(angle)


def line_twist():
    return np.stack(turn(np.arange(32)[:, None] * np.arange(128), N)).astype(np.float32)


def row_constants():
    mats = []
    for kind in range(4):
        k2 = np.array([[member(kind, g, s) for s in range(4)] for g in range(32)])
        cosine, sine = turn(k2[:, :, None] * np.arange(128), 128)
        real = np.concatenate([cosine, sine], -1)
        imag = np.concatenate([-sine, cosine], -1)
        both = np.stack([real.reshape(32, 2, 2, 256), imag.reshape(32, 2, 2, 256)], 2)
        mats.append(halves(both.reshape(256, 256)))
    return np.stack(mats), line_twist()


def column_constants():
    cosine, sine = turn(np.arange(16)[:, None] * np.arange(16), 16)
    eye8 = np.eye(8)
    forward = np.block(
        [
            [np.kron(eye8, cosine), np.kron(eye8, -sine)],
            [np.kron(eye8, sine), np.kron(eye8, cosine)],
        ]
    )
    pick = np.kron(np.ones((2, 2)), np.eye(4))

    def spread(block):
        return np.kron(pick, block)

    inverse = np.block([[spread(cosine), spread(sine)], [spread(-sine), spread(cosine)]])
    lane = np.arange(128)
    within = lane % 16
    top = lane // 64
    parity = np.arange(2)[:, None, None]
    ahead = np.stack(turn((2 * np.arange(128)[None, :, None] + parity) * within, N))
    steps = np.arange(64)[None, :, None]
    behind = [
        turn((2 * steps + parity + 128 * h) * within + (32 * steps + 2048 * h) * top, N)
        for h in range(2)
    ]
    spin = np.stack(turn(2 * np.arange(64)[:, None] + top, 256)).astype(np.float32)
    ahead, behind = ahead.astype(np.float32), np.stack(behind).astype(np.float32)
    return np.concatenate([halves(forward), halves(inverse)]), ahead, behind, spin


def image_constants():
    mats = []
    for kind in range(4):
        k2 = np.array([[member(kind, g, s) for g in range(32)] for s in range(4)])
        k2 = k2.reshape(2, 2, 32).transpose(0, 2, 1).reshape(2, 64)
        cosine, sine = turn(k2[:, :, None] * np.arange(128), 128)
        real = np.concatenate([cosine, sine], -1)
        imag = np.concatenate([-sine, cosine], -1)
        mats.append(halves(np.stack([real, imag], 1).reshape(256, 256) * (0.5 / (N * N))))
    return np.stack(mats), line_twist()


def turned(value, angle_index, length, sign):
    angle_index %= length
    real, imag = value
    if angle_index == 0:
        return value
    if 4 * angle_index == length:
        return (-imag, real) if sign > 0 else (imag, -real)
    if 2 * angle_index == length:
        return (-real, -imag)
    if 4 * angle_index == 3 * length:
        return (imag, -real) if sign > 0 else (-imag, real)
    angle = sign * 2.0 * math.pi * angle_index / length
    cosine, sine = math.cos(angle), math.sin(angle)
    if (8 * angle_index) % length == 0:
        scale = abs(cosine)
        plus, minus = (real + imag) * scale, (real - imag) * scale
        if cosine > 0:
            return (minus, plus) if sine > 0 else (plus, -minus)
        return (-plus, minus) if sine > 0 else (-minus, -plus)
    return (real * cosine - imag * sine, imag * cosine + real * sine)


def plus(a, b):
    return (a[0] + b[0], a[1] + b[1])


def minus(a, b):
    return (a[0] - b[0], a[1] - b[1])


def transform(values, sign):
    length = len(values)
    if length == 1:
        return values
    if length == 2:
        return [plus(values[0], values[1]), minus(values[0], values[1])]
    quarter = length // 4
    columns = []
    for b in range(quarter):
        z0, z1, z2, z3 = (values[a * quarter + b] for a in range(4))
        even, odd = plus(z0, z2), plus(z1, z3)
        even_gap, odd_gap = minus(z0, z2), turned(minus(z1, z3), 1, 4, sign)
        outs = [plus(even, odd), plus(even_gap, odd_gap), minus(even, odd), minus(even_gap, odd_gap)]
        columns.append([turned(z, b * k, length, sign) for k, z in enumerate(outs)])
    result = [None] * length
    for k in range(4):
        for m, z in enumerate(transform([columns[b][k] for b in range(quarter)], sign)):
            result[k + 4 * m] = z
    return result


def times(value, cosine, sine):
    real, imag = value
    return (real * cosine - imag * sine, imag * cosine + real * sine)


def split(value):
    high = value.astype(BF16)
    return high, (value - high.astype(F32)).astype(BF16)


def product(left, right, dims):
    def one(a, b):
        return lax.dot_general(a, b, (dims, ((), ())), preferred_element_type=F32)

    return one(left[0], right[0]) + (one(left[0], right[1]) + one(left[1], right[0]))


def rows_kernel(field_ref, mats_ref, twist_ref, out_ref, high_ref, low_ref):
    for j in range(2):
        lines = []
        for n1 in range(32):
            at = pl.ds(128 * (n1 % 4), 128)
            lines.append(
                (field_ref[n1 // 4, 2 * j, :, at], field_ref[n1 // 4, 2 * j + 1, :, at])
            )
        lines = transform(lines, -1)
        for k1, line in enumerate(lines):
            if k1:
                line = times(line, twist_ref[0, pl.ds(k1, 1), :], -twist_ref[1, pl.ds(k1, 1), :])
            place = k1 if k1 < 16 else 16 + ((32 - k1) % 16 ^ 2)
            rows = pl.ds(128 * (place // 4) + 64 * j + 16 * (place % 4), 16)
            for part in range(2):
                high, low = split(line[part])
                high_ref[rows, pl.ds(128 * part, 128)] = high
                low_ref[rows, pl.ds(128 * part, 128)] = low

    def mixed(kind, start, count):
        rows = pl.ds(start, count)
        data = (high_ref[rows, :], low_ref[rows, :])
        return product((mats_ref[kind, 0], mats_ref[kind, 1]), data, ((1,), (1,)))

    lane = lax.broadcasted_iota(jnp.int32, (256, 128), 1)
    for half in range(2):
        positive, negative = mixed(POS, 256 * half, 256), mixed(NEG, 512 + 256 * half, 256)
        for pair in range(2):
            at = slice(128 * pair, 128 * pair + 128)
            one, two = positive[:, at], negative[:, at]
            low = (lane & 32) == 0
            even, odd = jnp.where(low, one, two), jnp.where(low, two, one)
            if half == 0 and pair == 0:
                even = jnp.where((lane & 48) == 0, mixed(ZERO, 0, 128), even)
                even = jnp.where((lane & 48) == 32, mixed(HALF, 512, 128), even)
            for side, block in enumerate([even, odd]):
                quad = 4 * half + 2 * pair + side
                out_ref[pl.ds(32 * quad, 32)] = block.reshape(32, 8, 128)


def sine_turns(turns):
    t = turns - jnp.round(turns)
    square = t * t
    total = SINE[-1]
    for coefficient in SINE[-2::-1]:
        total = total * square + coefficient
    return total * t


def sine_fit():
    nodes = np.cos(np.pi * (np.arange(400) + 0.5) / 800) * 0.5
    basis = np.stack([nodes ** (2 * k + 1) for k in range(6)], 1)
    return [float(c) for c in np.linalg.lstsq(basis, np.sin(2 * np.pi * nodes), rcond=None)[0]]


SINE = sine_fit()


def device_number():
    n = 8 * lax.axis_index("row") + lax.axis_index("col")
    return 2 * (n % 128) + n // 128


def arc_tangent(value):
    for _ in range(2):
        value = value / (1.0 + jnp.sqrt(1.0 + value * value))
    square = value * value
    total = 1.0 / 17.0
    for k in range(15, 0, -2):
        total = 1.0 / k - square * total
    return 4.0 * value * total


def columns_kernel(
    fresnel_ref,
    terms_ref,
    field_ref,
    mats_hbm,
    ahead_hbm,
    behind_hbm,
    spin_hbm,
    out_ref,
    work_ref,
    back_ref,
    mats_ref,
    ahead_ref,
    behind_ref,
    spin_ref,
    sems,
):
    copies = [
        pltpu.make_async_copy(source, target, sems.at[k])
        for k, (source, target) in enumerate(
            [
                (mats_hbm, mats_ref),
                (ahead_hbm, ahead_ref),
                (behind_hbm, behind_ref),
                (spin_hbm, spin_ref),
            ]
        )
    ]
    for copy in copies:
        copy.start()
    device = device_number()
    quad, group = device // 32, device % 32
    sub = lax.broadcasted_iota(jnp.int32, (8, 128), 0)
    lane = lax.broadcasted_iota(jnp.int32, (8, 128), 1)
    first = (sub & 2) == 0
    sign = jnp.where(first, 1.0, -1.0).astype(F32)

    def shift(value, amount, axis):
        return pltpu.roll(value, amount, axis + value.ndim - 2)

    def swap_pairs(value):
        return jnp.where(first, shift(value, 6, 0), shift(value, 2, 0))

    for nb in range(8):
        lines = []
        for na in range(16):
            n = 8 * na + nb
            one, two = field_ref[2 * n], field_ref[2 * n + 1]
            one, two = one + two, one - two
            line = (jnp.where(first, one, shift(two, 2, 0)), jnp.where(first, shift(one, 6, 0), two))
            if n:
                angle = 2.0 * math.pi * n / 256
                line = times(
                    line,
                    jnp.where(first, 1.0, math.cos(angle)).astype(F32),
                    jnp.where(first, 0.0, -math.sin(angle)).astype(F32),
                )
            lines.append(line)
        for ka, line in enumerate(transform(lines, -1)):
            real, imag = turned(line, nb * ka, 128, -1)
            work_ref[0, ka, nb] = real
            work_ref[1, ka, nb] = imag

    slot = ((lane >> 4) & 3) ^ (2 * (quad & 1))
    s = ((sub >> 2) << 1) | (sub & 1)
    positive = 4 * group + s
    base = 2 * group + (s & 1)
    mirrored = jnp.where(s < 2, base, jnp.where(base == 0, 64, 128 - base))
    halfway = jnp.where(s < 2, base, 127 - base)
    k2 = jnp.where(slot < 2, positive, 127 - positive)
    k1 = 2 * quad + (slot & 1)
    k1 = jnp.where(slot < 2, k1, 32 - k1)
    special = (quad == 0) & ((slot & 1) == 0)
    k2 = jnp.where(special, jnp.where(slot == 0, mirrored, halfway), k2)
    k1 = jnp.where(special, jnp.where(slot == 0, 0, 16), k1)
    v = k1 + 32 * k2
    v = jnp.where(v >= N // 2, v - N, v).astype(F32)
    v_square = v * v
    a2 = lane & 15
    u_base = (((sub >> 1) & 1) + 256 * a2 - jnp.where(a2 >= 8, N, 0)).astype(F32)
    later = lane >= 64
    rate_even = (0.5 / (N * N)) / jnp.where(later, fresnel_ref[2], fresnel_ref[0])
    rate_odd = (0.5 / (N * N)) / jnp.where(later, fresnel_ref[3], fresnel_ref[1])
    ratio = jnp.full((8, 128), terms_ref[0], F32)
    offset = arc_tangent(ratio) * (0.5 / math.pi)
    gain = 2.0 * jnp.sqrt(1.0 + ratio * ratio)
    floor = terms_ref[1]

    def rows_of(table, which, start, count, stride):
        picked = []
        for part in range(2):
            tiles = []
            for k in range(count):
                at = pl.ds(start + stride * k, 1)
                upper = jnp.broadcast_to(table[which + (part, 0, at)], (8, 128))
                lower = jnp.broadcast_to(table[which + (part, 1, at)], (8, 128))
                tiles.append(jnp.where(first, upper, lower))
            picked.append(jnp.stack(tiles))
        return picked

    for copy in copies:
        copy.wait()
    forward = (mats_ref[0], mats_ref[1])
    inverse = (mats_ref[2], mats_ref[3])
    natural = ((1,), (0,))
    for bunch in range(4):
        reals, imags = [], []
        for ka in range(4 * bunch, 4 * bunch + 4):
            lines = transform([(work_ref[0, ka, nb], work_ref[1, ka, nb]) for nb in range(8)], -1)
            real = jnp.stack([z[0] for z in lines])
            imag = jnp.stack([z[1] for z in lines])
            cosine, sine = rows_of(ahead_ref, (), ka, 8, 16)
            real, imag = times((real, imag), cosine, -sine)
            reals.append(real.reshape(64, 128))
            imags.append(imag.reshape(64, 128))
        mixed = jnp.concatenate(
            [jnp.concatenate(reals, 0), jnp.concatenate(imags, 0)], 1
        )
        mixed = product(split(mixed), forward, natural)
        reals, imags = [], []
        for step in range(4):
            ka = 4 * bunch + step
            rows = slice(64 * step, 64 * step + 64)
            real = mixed[rows, :128].reshape(8, 8, 128)
            imag = mixed[rows, 128:].reshape(8, 8, 128)
            w1 = 2 * ka + 32 * lax.broadcasted_iota(jnp.int32, (8, 8, 128), 0)
            u = u_base + w1.astype(F32)
            radius = u * u + v_square
            even = gain * sine_turns(radius * rate_even + offset)
            odd = gain * sine_turns(radius * rate_odd + offset)
            energy = even * even + odd * odd
            scale = 1.0 / (energy + shift(energy, 64, 1) + floor)
            reals.append(((even * real + odd * imag) * scale).reshape(64, 128))
            imags.append(((even * imag - odd * real) * scale).reshape(64, 128))
        mixed = jnp.concatenate(
            [jnp.concatenate(reals, 0), jnp.concatenate(imags, 0)], 1
        )
        mixed = product(split(mixed), inverse, natural)
        for step in range(4):
            ka = 4 * bunch + step
            rows = slice(64 * step, 64 * step + 64)
            real = mixed[rows, :128].reshape(8, 8, 128)
            imag = mixed[rows, 128:].reshape(8, 8, 128)
            early = times((real[:4], imag[:4]), *rows_of(behind_ref, (0,), ka, 4, 16))
            later_half = times((real[4:], imag[4:]), *rows_of(behind_ref, (1,), ka, 4, 16))
            real, imag = plus(early, later_half)
            back_ref[0, ka] = real
            back_ref[1, ka] = imag

    for wb in range(8):
        lines = [
            tuple(back_ref[part, wb + 8 * (wa % 2), wa // 2] for part in range(2)) for wa in range(8)
        ]
        for na, line in enumerate(transform(lines, 1)):
            real, imag = turned(line, wb * na, 64, 1)
            work_ref[0, na, wb] = real
            work_ref[1, na, wb] = imag
    bit5 = (lane & 32) != 0
    reflected = (quad == 0) & ((lane & 16) == 0)
    itself = (quad == 0) & (group == 0) & ((lane & 48) == 0) & ((sub & 1) == 0)
    low_half = (lane & 8) == 0
    straight = ((sub & 4) != 0) == (lane >= 64)

    def partner(value):
        across = jnp.where(bit5, shift(value, 32, 1), shift(value, 96, 1))
        down = jnp.where(itself, value, shift(value, 4, 0))
        return jnp.where(reflected, down, across)

    for na in range(8):
        lines = [(work_ref[0, na, wb], work_ref[1, na, wb]) for wb in range(8)]
        for nb, line in enumerate(transform(lines, 1)):
            at = pl.ds(na + 8 * nb, 1)
            cosine, sine = (jnp.broadcast_to(spin_ref[part, at], (8, 128)) for part in range(2))
            line = times(line, jnp.where(first, 1.0, cosine), jnp.where(first, 0.0, sine))
            real, imag = (swap_pairs(z) + sign * z for z in line)
            real, imag = real + partner(real), imag - partner(imag)
            packed = real + jnp.where(low_half, -shift(imag, 120, 1), shift(imag, 8, 1))
            crossed = shift(shift(packed, 64, 1), 4, 0)
            out_ref[na + 8 * nb] = jnp.where(straight, packed, crossed)


def image_kernel(field_ref, mats_ref, twist_ref, out_ref):
    lane = lax.broadcasted_iota(jnp.int32, (64, 128), 1)
    bit6, bit3 = (lane & 64) != 0, (lane & 8) != 0
    tiles = {}
    for half in range(2):
        quads = [field_ref[pl.ds(256 * half + 64 * q, 64), :] for q in range(4)]
        parts = []
        for qb in range(2):
            one, two = quads[qb], quads[2 + qb]
            parts.append(
                (
                    jnp.where(bit6, pltpu.roll(two, 64, 1), one),
                    jnp.where(bit6, two, pltpu.roll(one, 64, 1)),
                )
            )
        stacked = []
        for s1 in range(2):
            one, two = parts[0][s1], parts[1][s1]
            stacked.append(jnp.where(bit3, pltpu.roll(two, 8, 1), one))
            stacked.append(jnp.where(bit3, two, pltpu.roll(one, 120, 1)))
        lines = jnp.concatenate(stacked, 0).T
        for q in range(4):
            for slot, k1 in enumerate(residues(4 * half + q)):
                start = 64 * (q // 2) + 16 * slot + 8 * (q % 2)
                tiles[k1] = lines[start : start + 8]
    lines = {}
    for kind, members in (
        (POS, [1, *range(1, 16)]),
        (NEG, [17, *range(17, 32)]),
        (ZERO, [0, 0]),
        (HALF, [16, 16]),
    ):
        data = split(jnp.concatenate([tiles[k1] for k1 in members], 0))
        value = product(data, (mats_ref[kind, 0], mats_ref[kind, 1]), ((1,), (0,)))
        for k, k1 in enumerate(members):
            line = (value[8 * k : 8 * k + 8, :128], value[8 * k : 8 * k + 8, 128:])
            lines[k1] = times(line, twist_ref[0, pl.ds(k1, 1), :], twist_ref[1, pl.ds(k1, 1), :])
    for n1, (real, imag) in enumerate(transform([lines[k1] for k1 in range(32)], 1)):
        at = pl.ds(128 * (n1 % 4), 128)
        out_ref[n1 // 4, pl.ds(0, 8), at] = real
        out_ref[n1 // 4, pl.ds(8, 8), at] = imag


def call(kernel, out_shape, scratch, arguments, spaces):
    return pl.pallas_call(
        kernel,
        out_shape=jax.ShapeDtypeStruct(out_shape, F32),
        in_specs=[pl.BlockSpec(memory_space=space) for space in spaces],
        out_specs=pl.BlockSpec(memory_space=pltpu.VMEM),
        scratch_shapes=scratch,
        compiler_params=pltpu.CompilerParams(vmem_limit_bytes=40 * 1024 * 1024),
    )(*arguments)


def image_rows(field):
    arguments = [field] + [jnp.asarray(c) for c in row_constants()]
    scratch = [pltpu.VMEM((1024, 256), BF16), pltpu.VMEM((1024, 256), BF16)]
    return call(rows_kernel, (256, 8, 128), scratch, arguments, [pltpu.VMEM] * 3)


def filter_columns(field, fresnel, ctf_terms):
    constants = [jnp.asarray(c) for c in column_constants()]
    scratch = [pltpu.VMEM((2, 16, 8, 8, 128), F32), pltpu.VMEM((2, 16, 4, 8, 128), F32)]
    scratch += [pltpu.VMEM(c.shape, c.dtype) for c in constants] + [pltpu.SemaphoreType.DMA((4,))]
    spaces = [pltpu.SMEM] * 2 + [pltpu.VMEM] + [pltpu.HBM] * 4
    arguments = [fresnel, ctf_terms, field] + constants
    return call(columns_kernel, (64, 8, 128), scratch, arguments, spaces)


def image_from(field):
    arguments = [field] + [jnp.asarray(c) for c in image_constants()]
    return call(image_kernel, (8, 16, 512), [], arguments, [pltpu.VMEM] * 3)


def exchange(field):
    return lax.all_to_all(field, "col", split_axis=0, concat_axis=0, tiled=True)


def exchange_all(field):
    return lax.all_to_all(
        field, ("row", "col"), split_axis=0, concat_axis=0, tiled=True, axis_index_groups=[ORDER]
    )


def local(holograms, fresnel, ctf_terms):
    field = holograms.reshape(4, 8, 16, 512).transpose(1, 0, 2, 3)
    field = image_rows(exchange(field))
    field = filter_columns(exchange_all(field), fresnel, ctf_terms)
    field = exchange_all(field.reshape(256, 2, 128))
    image = image_from(field.reshape(512, 128))
    return exchange(image).reshape(128, 512)


def solution(mesh):
    in_specs = (P(None, "row", "col"), P(), P())
    out_specs = P("row", "col")
    return jax.shard_map(local, mesh=mesh, in_specs=in_specs, out_specs=out_specs, check_vma=False)
```

```python
import math

import jax
import jax.numpy as jnp
import ml_dtypes
import numpy as np
from jax import lax
from jax.experimental import pallas as pl
from jax.experimental.pallas import tpu as pltpu
from jax.sharding import PartitionSpec as P

N = 4096
POS, NEG, ZERO, HALF = range(4)
ORDER = [128 * (place % 2) + place // 2 for place in range(256)]
F32 = jnp.float32
BF16 = jnp.bfloat16


def residues(quad):
    low, high = 2 * quad, 2 * quad + 1
    if quad == 0:
        return [0, 1, 16, 31]
    if quad % 2:
        return [32 - low, 32 - high, low, high]
    return [low, high, 32 - low, 32 - high]


def member(kind, group, slot):
    if kind == POS:
        return 4 * group + slot
    if kind == NEG:
        return 127 - 4 * group - slot
    if kind == ZERO:
        return [2 * group, 2 * group + 1, 128 - 2 * group if group else 64, 127 - 2 * group][slot]
    return [2 * group, 2 * group + 1, 127 - 2 * group, 126 - 2 * group][slot]


def halves(matrix):
    high = matrix.astype(ml_dtypes.bfloat16)
    low = (matrix - high.astype(np.float64)).astype(ml_dtypes.bfloat16)
    return np.stack([high, low])


def turn(product, length):
    angle = 2.0 * np.pi * (np.asarray(product, np.int64) % length) / length
    return np.cos(angle), np.sin(angle)


def line_twist():
    return np.stack(turn(np.arange(32)[:, None] * np.arange(128), N)).astype(np.float32)


def row_constants():
    mats = []
    for kind in range(4):
        k2 = np.array([[member(kind, g, s) for s in range(4)] for g in range(32)])
        cosine, sine = turn(k2[:, :, None] * np.arange(128), 128)
        real = np.concatenate([cosine, sine], -1)
        imag = np.concatenate([-sine, cosine], -1)
        both = np.stack([real.reshape(32, 2, 2, 256), imag.reshape(32, 2, 2, 256)], 2)
        mats.append(halves(both.reshape(256, 256)))
    return np.stack(mats), line_twist()


def column_constants():
    cosine, sine = turn(np.arange(16)[:, None] * np.arange(16), 16)
    eye8 = np.eye(8)
    forward = np.block(
        [
            [np.kron(eye8, cosine), np.kron(eye8, -sine)],
            [np.kron(eye8, sine), np.kron(eye8, cosine)],
        ]
    )
    pick = np.kron(np.ones((2, 2)), np.eye(4))

    def spread(block):
        return np.kron(pick, block)

    inverse = np.block([[spread(cosine), spread(sine)], [spread(-sine), spread(cosine)]])
    lane = np.arange(128)
    within = lane % 16
    top = lane // 64
    parity = np.arange(2)[:, None, None]
    ahead = np.stack(turn((2 * np.arange(128)[None, :, None] + parity) * within, N))
    steps = np.arange(64)[None, :, None]
    behind = [
        turn((2 * steps + parity + 128 * h) * within + (32 * steps + 2048 * h) * top, N)
        for h in range(2)
    ]
    spin = np.stack(turn(2 * np.arange(64)[:, None] + top, 256)).astype(np.float32)
    ahead = np.repeat(ahead[:, [0, 1, 0, 1]].transpose(0, 2, 1, 3), 2, 2)
    ahead, behind = ahead.astype(np.float32), np.stack(behind).astype(np.float32)
    return np.concatenate([halves(forward), halves(inverse)]), ahead, behind, spin


def image_constants():
    mats = []
    for kind in range(4):
        k2 = np.array([[member(kind, g, s) for g in range(32)] for s in range(4)])
        k2 = k2.reshape(2, 2, 32).transpose(0, 2, 1).reshape(2, 64)
        cosine, sine = turn(k2[:, :, None] * np.arange(128), 128)
        real = np.concatenate([cosine, sine], -1)
        imag = np.concatenate([-sine, cosine], -1)
        mats.append(halves(np.stack([real, imag], 1).reshape(256, 256) * (0.5 / (N * N))))
    return np.stack(mats), line_twist()


def turned(value, angle_index, length, sign):
    angle_index %= length
    real, imag = value
    if angle_index == 0:
        return value
    if 4 * angle_index == length:
        return (-imag, real) if sign > 0 else (imag, -real)
    if 2 * angle_index == length:
        return (-real, -imag)
    if 4 * angle_index == 3 * length:
        return (imag, -real) if sign > 0 else (-imag, real)
    angle = sign * 2.0 * math.pi * angle_index / length
    cosine, sine = math.cos(angle), math.sin(angle)
    if (8 * angle_index) % length == 0:
        scale = abs(cosine)
        plus, minus = (real + imag) * scale, (real - imag) * scale
        if cosine > 0:
            return (minus, plus) if sine > 0 else (plus, -minus)
        return (-plus, minus) if sine > 0 else (-minus, -plus)
    return (real * cosine - imag * sine, imag * cosine + real * sine)


def plus(a, b):
    return (a[0] + b[0], a[1] + b[1])


def minus(a, b):
    return (a[0] - b[0], a[1] - b[1])


def transform(values, sign):
    length = len(values)
    if length == 1:
        return values
    if length == 2:
        return [plus(values[0], values[1]), minus(values[0], values[1])]
    quarter = length // 4
    columns = []
    for b in range(quarter):
        z0, z1, z2, z3 = (values[a * quarter + b] for a in range(4))
        even, odd = plus(z0, z2), plus(z1, z3)
        even_gap, odd_gap = minus(z0, z2), turned(minus(z1, z3), 1, 4, sign)
        outs = [plus(even, odd), plus(even_gap, odd_gap), minus(even, odd), minus(even_gap, odd_gap)]
        columns.append([turned(z, b * k, length, sign) for k, z in enumerate(outs)])
    result = [None] * length
    for k in range(4):
        for m, z in enumerate(transform([columns[b][k] for b in range(quarter)], sign)):
            result[k + 4 * m] = z
    return result


def times(value, cosine, sine):
    real, imag = value
    return (real * cosine - imag * sine, imag * cosine + real * sine)


def split(value):
    high = value.astype(BF16)
    return high, (value - high.astype(F32)).astype(BF16)


def product(left, right, dims):
    def one(a, b):
        return lax.dot_general(a, b, (dims, ((), ())), preferred_element_type=F32)

    return one(left[0], right[0]) + (one(left[0], right[1]) + one(left[1], right[0]))


def rows_kernel(field_ref, mats_ref, twist_ref, out_ref, high_ref, low_ref):
    for j in range(2):
        lines = []
        for n1 in range(32):
            at = pl.ds(128 * (n1 % 4), 128)
            lines.append(
                (field_ref[n1 // 4, 2 * j, :, at], field_ref[n1 // 4, 2 * j + 1, :, at])
            )
        lines = transform(lines, -1)
        for k1, line in enumerate(lines):
            if k1:
                line = times(line, twist_ref[0, pl.ds(k1, 1), :], -twist_ref[1, pl.ds(k1, 1), :])
            place = k1 if k1 < 16 else 16 + ((32 - k1) % 16 ^ 2)
            rows = pl.ds(128 * (place // 4) + 64 * j + 16 * (place % 4), 16)
            for part in range(2):
                high, low = split(line[part])
                high_ref[rows, pl.ds(128 * part, 128)] = high
                low_ref[rows, pl.ds(128 * part, 128)] = low

    def mixed(kind, start, count):
        rows = pl.ds(start, count)
        data = (high_ref[rows, :], low_ref[rows, :])
        return product((mats_ref[kind, 0], mats_ref[kind, 1]), data, ((1,), (1,)))

    lane = lax.broadcasted_iota(jnp.int32, (256, 128), 1)
    for half in range(2):
        positive, negative = mixed(POS, 256 * half, 256), mixed(NEG, 512 + 256 * half, 256)
        for pair in range(2):
            at = slice(128 * pair, 128 * pair + 128)
            one, two = positive[:, at], negative[:, at]
            low = (lane & 32) == 0
            even, odd = jnp.where(low, one, two), jnp.where(low, two, one)
            if half == 0 and pair == 0:
                even = jnp.where((lane & 48) == 0, mixed(ZERO, 0, 128), even)
                even = jnp.where((lane & 48) == 32, mixed(HALF, 512, 128), even)
            for side, block in enumerate([even, odd]):
                quad = 4 * half + 2 * pair + side
                out_ref[pl.ds(32 * quad, 32)] = block.reshape(32, 8, 128)


def sine_turns(turns):
    t = turns - jnp.round(turns)
    square = t * t
    total = SINE[-1]
    for coefficient in SINE[-2::-1]:
        total = total * square + coefficient
    return total * t


def sine_fit():
    nodes = np.cos(np.pi * (np.arange(400) + 0.5) / 800) * 0.5
    basis = np.stack([nodes ** (2 * k + 1) for k in range(6)], 1)
    return [float(c) for c in np.linalg.lstsq(basis, np.sin(2 * np.pi * nodes), rcond=None)[0]]


SINE = sine_fit()


def device_number():
    n = 8 * lax.axis_index("row") + lax.axis_index("col")
    return 2 * (n % 128) + n // 128


def arc_tangent(value):
    for _ in range(2):
        value = value / (1.0 + jnp.sqrt(1.0 + value * value))
    square = value * value
    total = 1.0 / 17.0
    for k in range(15, 0, -2):
        total = 1.0 / k - square * total
    return 4.0 * value * total


def columns_kernel(
    fresnel_ref,
    terms_ref,
    field_ref,
    mats_ref,
    ahead_ref,
    behind_ref,
    spin_ref,
    out_ref,
    work_ref,
    back_ref,
):
    device = device_number()
    quad, group = device // 32, device % 32
    sub = lax.broadcasted_iota(jnp.int32, (8, 128), 0)
    lane = lax.broadcasted_iota(jnp.int32, (8, 128), 1)
    first = (sub & 2) == 0
    sign = jnp.where(first, 1.0, -1.0).astype(F32)

    def shift(value, amount, axis):
        return pltpu.roll(value, amount, axis + value.ndim - 2)

    def swap_pairs(value):
        return jnp.where(first, shift(value, 6, 0), shift(value, 2, 0))

    for nb in range(8):
        lines = []
        for na in range(16):
            n = 8 * na + nb
            one, two = field_ref[2 * n], field_ref[2 * n + 1]
            one, two = one + two, one - two
            line = (jnp.where(first, one, shift(two, 2, 0)), jnp.where(first, shift(one, 6, 0), two))
            if n:
                angle = 2.0 * math.pi * n / 256
                line = times(
                    line,
                    jnp.where(first, 1.0, math.cos(angle)).astype(F32),
                    jnp.where(first, 0.0, -math.sin(angle)).astype(F32),
                )
            lines.append(line)
        for ka, line in enumerate(transform(lines, -1)):
            real, imag = turned(line, nb * ka, 128, -1)
            work_ref[0, ka, nb] = real
            work_ref[1, ka, nb] = imag

    slot = ((lane >> 4) & 3) ^ (2 * (quad & 1))
    s = ((sub >> 2) << 1) | (sub & 1)
    positive = 4 * group + s
    base = 2 * group + (s & 1)
    mirrored = jnp.where(s < 2, base, jnp.where(base == 0, 64, 128 - base))
    halfway = jnp.where(s < 2, base, 127 - base)
    k2 = jnp.where(slot < 2, positive, 127 - positive)
    k1 = 2 * quad + (slot & 1)
    k1 = jnp.where(slot < 2, k1, 32 - k1)
    special = (quad == 0) & ((slot & 1) == 0)
    k2 = jnp.where(special, jnp.where(slot == 0, mirrored, halfway), k2)
    k1 = jnp.where(special, jnp.where(slot == 0, 0, 16), k1)
    v = k1 + 32 * k2
    v = jnp.where(v >= N // 2, v - N, v).astype(F32)
    v_square = v * v
    a2 = lane & 15
    u_base = (((sub >> 1) & 1) + 256 * a2 - jnp.where(a2 >= 8, N, 0)).astype(F32)
    later = lane >= 64
    rate_even = (0.5 / (N * N)) / jnp.where(later, fresnel_ref[2], fresnel_ref[0])
    rate_odd = (0.5 / (N * N)) / jnp.where(later, fresnel_ref[3], fresnel_ref[1])
    ratio = jnp.full((8, 128), terms_ref[0], F32)
    offset = arc_tangent(ratio) * (0.5 / math.pi)
    gain = 2.0 * jnp.sqrt(1.0 + ratio * ratio)
    floor = terms_ref[1] / gain

    def rows_of(table, which, start, count, stride):
        picked = []
        for part in range(2):
            tiles = []
            for k in range(count):
                at = pl.ds(start + stride * k, 1)
                upper = jnp.broadcast_to(table[which + (part, 0, at)], (8, 128))
                lower = jnp.broadcast_to(table[which + (part, 1, at)], (8, 128))
                tiles.append(jnp.where(first, upper, lower))
            picked.append(jnp.stack(tiles))
        return picked

    forward = (mats_ref[0], mats_ref[1])
    inverse = (mats_ref[2], mats_ref[3])
    natural = ((1,), (0,))
    for bunch in range(4):
        reals, imags = [], []
        for ka in range(4 * bunch, 4 * bunch + 4):
            lines = transform([(work_ref[0, ka, nb], work_ref[1, ka, nb]) for nb in range(8)], -1)
            real = jnp.stack([z[0] for z in lines])
            imag = jnp.stack([z[1] for z in lines])
            cosine, sine = (
                jnp.stack([ahead_ref[part, ka + 16 * kb] for kb in range(8)]) for part in range(2)
            )
            real, imag = times((real, imag), cosine, -sine)
            reals.append(real.reshape(64, 128))
            imags.append(imag.reshape(64, 128))
        mixed = jnp.concatenate(
            [jnp.concatenate(reals, 0), jnp.concatenate(imags, 0)], 1
        )
        mixed = product(split(mixed), forward, natural)
        reals, imags = [], []
        for step in range(4):
            ka = 4 * bunch + step
            rows = slice(64 * step, 64 * step + 64)
            real = mixed[rows, :128].reshape(8, 8, 128)
            imag = mixed[rows, 128:].reshape(8, 8, 128)
            for kb in range(8):
                u = u_base + float(2 * ka + 32 * kb)
                radius = u * u + v_square
                even = sine_turns(radius * rate_even + offset)
                odd = sine_turns(radius * rate_odd + offset)
                energy = even * even + odd * odd
                scale = 1.0 / (gain * (energy + shift(energy, 64, 1)) + floor)
                reals.append((even * real[kb] + odd * imag[kb]) * scale)
                imags.append((even * imag[kb] - odd * real[kb]) * scale)
        mixed = jnp.concatenate(
            [jnp.concatenate(reals, 0), jnp.concatenate(imags, 0)], 1
        )
        mixed = product(split(mixed), inverse, natural)
        for step in range(4):
            ka = 4 * bunch + step
            rows = slice(64 * step, 64 * step + 64)
            real = mixed[rows, :128].reshape(8, 8, 128)
            imag = mixed[rows, 128:].reshape(8, 8, 128)
            early = times((real[:4], imag[:4]), *rows_of(behind_ref, (0,), ka, 4, 16))
            later_half = times((real[4:], imag[4:]), *rows_of(behind_ref, (1,), ka, 4, 16))
            real, imag = plus(early, later_half)
            back_ref[0, ka] = real
            back_ref[1, ka] = imag

    for wb in range(8):
        lines = [
            tuple(back_ref[part, wb + 8 * (wa % 2), wa // 2] for part in range(2)) for wa in range(8)
        ]
        for na, line in enumerate(transform(lines, 1)):
            real, imag = turned(line, wb * na, 64, 1)
            work_ref[0, na, wb] = real
            work_ref[1, na, wb] = imag
    bit5 = (lane & 32) != 0
    reflected = (quad == 0) & ((lane & 16) == 0)
    itself = (quad == 0) & (group == 0) & ((lane & 48) == 0) & ((sub & 1) == 0)
    low_half = (lane & 8) == 0
    straight = ((sub & 4) != 0) == (lane >= 64)

    def partner(value):
        across = jnp.where(bit5, shift(value, 32, 1), shift(value, 96, 1))
        down = jnp.where(itself, value, shift(value, 4, 0))
        return jnp.where(reflected, down, across)

    for na in range(8):
        lines = [(work_ref[0, na, wb], work_ref[1, na, wb]) for wb in range(8)]
        for nb, line in enumerate(transform(lines, 1)):
            at = pl.ds(na + 8 * nb, 1)
            cosine, sine = (jnp.broadcast_to(spin_ref[part, at], (8, 128)) for part in range(2))
            line = times(line, jnp.where(first, 1.0, cosine), jnp.where(first, 0.0, sine))
            real, imag = (swap_pairs(z) + sign * z for z in line)
            real, imag = real + partner(real), imag - partner(imag)
            packed = real + jnp.where(low_half, -shift(imag, 120, 1), shift(imag, 8, 1))
            crossed = shift(shift(packed, 64, 1), 4, 0)
            out_ref[na + 8 * nb] = jnp.where(straight, packed, crossed)


def image_kernel(field_ref, mats_ref, twist_ref, out_ref):
    lane = lax.broadcasted_iota(jnp.int32, (64, 128), 1)
    bit6, bit3 = (lane & 64) != 0, (lane & 8) != 0
    tiles = {}
    for half in range(2):
        quads = [field_ref[pl.ds(256 * half + 64 * q, 64), :] for q in range(4)]
        parts = []
        for qb in range(2):
            one, two = quads[qb], quads[2 + qb]
            parts.append(
                (
                    jnp.where(bit6, pltpu.roll(two, 64, 1), one),
                    jnp.where(bit6, two, pltpu.roll(one, 64, 1)),
                )
            )
        stacked = []
        for s1 in range(2):
            one, two = parts[0][s1], parts[1][s1]
            stacked.append(jnp.where(bit3, pltpu.roll(two, 8, 1), one))
            stacked.append(jnp.where(bit3, two, pltpu.roll(one, 120, 1)))
        lines = jnp.concatenate(stacked, 0).T
        for q in range(4):
            for slot, k1 in enumerate(residues(4 * half + q)):
                start = 64 * (q // 2) + 16 * slot + 8 * (q % 2)
                tiles[k1] = lines[start : start + 8]
    lines = {}
    for kind, members in (
        (POS, [1, *range(1, 16)]),
        (NEG, [17, *range(17, 32)]),
        (ZERO, [0, 0]),
        (HALF, [16, 16]),
    ):
        data = split(jnp.concatenate([tiles[k1] for k1 in members], 0))
        value = product(data, (mats_ref[kind, 0], mats_ref[kind, 1]), ((1,), (0,)))
        for k, k1 in enumerate(members):
            line = (value[8 * k : 8 * k + 8, :128], value[8 * k : 8 * k + 8, 128:])
            lines[k1] = times(line, twist_ref[0, pl.ds(k1, 1), :], twist_ref[1, pl.ds(k1, 1), :])
    for n1, (real, imag) in enumerate(transform([lines[k1] for k1 in range(32)], 1)):
        at = pl.ds(128 * (n1 % 4), 128)
        out_ref[n1 // 4, pl.ds(0, 8), at] = real
        out_ref[n1 // 4, pl.ds(8, 8), at] = imag


def call(kernel, out_shape, scratch, arguments, spaces):
    return pl.pallas_call(
        kernel,
        out_shape=jax.ShapeDtypeStruct(out_shape, F32),
        in_specs=[pl.BlockSpec(memory_space=space) for space in spaces],
        out_specs=pl.BlockSpec(memory_space=pltpu.VMEM),
        scratch_shapes=scratch,
        compiler_params=pltpu.CompilerParams(vmem_limit_bytes=40 * 1024 * 1024),
    )(*arguments)


def image_rows(field):
    arguments = [field] + [jnp.asarray(c) for c in row_constants()]
    scratch = [pltpu.VMEM((1024, 256), BF16), pltpu.VMEM((1024, 256), BF16)]
    return call(rows_kernel, (256, 8, 128), scratch, arguments, [pltpu.VMEM] * 3)


def filter_columns(field, fresnel, ctf_terms):
    constants = [jnp.asarray(c) for c in column_constants()]
    scratch = [pltpu.VMEM((2, 16, 8, 8, 128), F32), pltpu.VMEM((2, 16, 4, 8, 128), F32)]
    spaces = [pltpu.SMEM] * 2 + [pltpu.VMEM] * 5
    arguments = [fresnel, ctf_terms, field] + constants
    return call(columns_kernel, (64, 8, 128), scratch, arguments, spaces)


def image_from(field):
    arguments = [field] + [jnp.asarray(c) for c in image_constants()]
    return call(image_kernel, (8, 16, 512), [], arguments, [pltpu.VMEM] * 3)


def exchange(field):
    return lax.all_to_all(field, "col", split_axis=0, concat_axis=0, tiled=True)


def exchange_all(field):
    return lax.all_to_all(
        field, ("row", "col"), split_axis=0, concat_axis=0, tiled=True, axis_index_groups=[ORDER]
    )


def local(holograms, fresnel, ctf_terms):
    field = holograms.reshape(4, 8, 16, 512).transpose(1, 0, 2, 3)
    field = image_rows(exchange(field))
    field = filter_columns(exchange_all(field), fresnel, ctf_terms)
    field = exchange_all(field.reshape(256, 2, 128))
    image = image_from(field.reshape(512, 128))
    return exchange(image).reshape(128, 512)


def solution(mesh):
    in_specs = (P(None, "row", "col"), P(), P())
    out_specs = P("row", "col")
    return jax.shard_map(local, mesh=mesh, in_specs=in_specs, out_specs=out_specs, check_vma=False)
```

```python
import math

import jax
import jax.numpy as jnp
import ml_dtypes
import numpy as np
from jax import lax
from jax.experimental import pallas as pl
from jax.experimental.pallas import tpu as pltpu
from jax.sharding import PartitionSpec as P

N = 4096
POS, NEG, ZERO, HALF = range(4)
ORDER = [128 * (place % 2) + place // 2 for place in range(256)]
F32 = jnp.float32
BF16 = jnp.bfloat16


def residues(quad):
    low, high = 2 * quad, 2 * quad + 1
    if quad == 0:
        return [0, 1, 16, 31]
    if quad % 2:
        return [32 - low, 32 - high, low, high]
    return [low, high, 32 - low, 32 - high]


def member(kind, group, slot):
    if kind == POS:
        return 4 * group + slot
    if kind == NEG:
        return 127 - 4 * group - slot
    if kind == ZERO:
        return [2 * group, 2 * group + 1, 128 - 2 * group if group else 64, 127 - 2 * group][slot]
    return [2 * group, 2 * group + 1, 127 - 2 * group, 126 - 2 * group][slot]


def halves(matrix):
    high = matrix.astype(ml_dtypes.bfloat16)
    low = (matrix - high.astype(np.float64)).astype(ml_dtypes.bfloat16)
    return np.stack([high, low])


def turn(product, length):
    angle = 2.0 * np.pi * (np.asarray(product, np.int64) % length) / length
    return np.cos(angle), np.sin(angle)


def line_twist():
    return np.stack(turn(np.arange(32)[:, None] * np.arange(128), N)).astype(np.float32)


def row_constants():
    mats = []
    for kind in range(4):
        k2 = np.array([[member(kind, g, s) for s in range(4)] for g in range(32)])
        cosine, sine = turn(k2[:, :, None] * np.arange(128), 128)
        real = np.concatenate([cosine, sine], -1)
        imag = np.concatenate([-sine, cosine], -1)
        both = np.stack([real.reshape(32, 2, 2, 256), imag.reshape(32, 2, 2, 256)], 2)
        mats.append(halves(both.reshape(256, 256)))
    return np.stack(mats), line_twist()


def column_constants():
    cosine, sine = turn(np.arange(16)[:, None] * np.arange(16), 16)
    eye8 = np.eye(8)
    forward = np.block(
        [
            [np.kron(eye8, cosine), np.kron(eye8, -sine)],
            [np.kron(eye8, sine), np.kron(eye8, cosine)],
        ]
    )
    pick = np.kron(np.ones((2, 2)), np.eye(4))

    def spread(block):
        return np.kron(pick, block)

    inverse = np.block([[spread(cosine), spread(sine)], [spread(-sine), spread(cosine)]])
    lane = np.arange(128)
    within = lane % 16
    top = lane // 64
    parity = np.arange(2)[:, None, None]
    ahead = np.stack(turn((2 * np.arange(128)[None, :, None] + parity) * within, N))
    steps = np.arange(64)[None, :, None]
    behind = [
        turn((2 * steps + parity + 128 * h) * within + (32 * steps + 2048 * h) * top, N)
        for h in range(2)
    ]
    spin = np.stack(turn(2 * np.arange(64)[:, None] + top, 256)).astype(np.float32)
    ahead = np.repeat(ahead[:, [0, 1, 0, 1]].transpose(0, 2, 1, 3), 2, 2)
    ahead, behind = ahead.astype(np.float32), np.stack(behind).astype(np.float32)
    return np.concatenate([halves(forward), halves(inverse)]), ahead, behind, spin


def image_constants():
    mats = []
    for kind in range(4):
        k2 = np.array([[member(kind, g, s) for g in range(32)] for s in range(4)])
        k2 = k2.reshape(2, 2, 32).transpose(0, 2, 1).reshape(2, 64)
        cosine, sine = turn(k2[:, :, None] * np.arange(128), 128)
        real = np.concatenate([cosine, sine], -1)
        imag = np.concatenate([-sine, cosine], -1)
        mats.append(halves(np.stack([real, imag], 1).reshape(256, 256) * (0.5 / (N * N))))
    return np.stack(mats), line_twist()


def turned(value, angle_index, length, sign):
    angle_index %= length
    real, imag = value
    if angle_index == 0:
        return value
    if 4 * angle_index == length:
        return (-imag, real) if sign > 0 else (imag, -real)
    if 2 * angle_index == length:
        return (-real, -imag)
    if 4 * angle_index == 3 * length:
        return (imag, -real) if sign > 0 else (-imag, real)
    angle = sign * 2.0 * math.pi * angle_index / length
    cosine, sine = math.cos(angle), math.sin(angle)
    if (8 * angle_index) % length == 0:
        scale = abs(cosine)
        plus, minus = (real + imag) * scale, (real - imag) * scale
        if cosine > 0:
            return (minus, plus) if sine > 0 else (plus, -minus)
        return (-plus, minus) if sine > 0 else (-minus, -plus)
    return (real * cosine - imag * sine, imag * cosine + real * sine)


def plus(a, b):
    return (a[0] + b[0], a[1] + b[1])


def minus(a, b):
    return (a[0] - b[0], a[1] - b[1])


def transform(values, sign):
    length = len(values)
    if length == 1:
        return values
    if length == 2:
        return [plus(values[0], values[1]), minus(values[0], values[1])]
    quarter = length // 4
    columns = []
    for b in range(quarter):
        z0, z1, z2, z3 = (values[a * quarter + b] for a in range(4))
        even, odd = plus(z0, z2), plus(z1, z3)
        even_gap, odd_gap = minus(z0, z2), turned(minus(z1, z3), 1, 4, sign)
        outs = [plus(even, odd), plus(even_gap, odd_gap), minus(even, odd), minus(even_gap, odd_gap)]
        columns.append([turned(z, b * k, length, sign) for k, z in enumerate(outs)])
    result = [None] * length
    for k in range(4):
        for m, z in enumerate(transform([columns[b][k] for b in range(quarter)], sign)):
            result[k + 4 * m] = z
    return result


def times(value, cosine, sine):
    real, imag = value
    return (real * cosine - imag * sine, imag * cosine + real * sine)


def split(value):
    high = value.astype(BF16)
    return high, (value - high.astype(F32)).astype(BF16)


def product(left, right, dims):
    def one(a, b):
        return lax.dot_general(a, b, (dims, ((), ())), preferred_element_type=F32)

    return one(left[0], right[0]) + (one(left[0], right[1]) + one(left[1], right[0]))


def rows_kernel(field_ref, mats_ref, twist_ref, out_ref, high_ref, low_ref):
    for j in range(2):
        lines = []
        for n1 in range(32):
            at = pl.ds(128 * (n1 % 4), 128)
            lines.append(
                (field_ref[n1 // 4, 2 * j, :, at], field_ref[n1 // 4, 2 * j + 1, :, at])
            )
        lines = transform(lines, -1)
        for k1, line in enumerate(lines):
            if k1:
                line = times(line, twist_ref[0, pl.ds(k1, 1), :], -twist_ref[1, pl.ds(k1, 1), :])
            place = k1 if k1 < 16 else 16 + ((32 - k1) % 16 ^ 2)
            rows = pl.ds(128 * (place // 4) + 64 * j + 16 * (place % 4), 16)
            for part in range(2):
                high, low = split(line[part])
                high_ref[rows, pl.ds(128 * part, 128)] = high
                low_ref[rows, pl.ds(128 * part, 128)] = low

    def mixed(kind, start, count):
        rows = pl.ds(start, count)
        data = (high_ref[rows, :], low_ref[rows, :])
        return product((mats_ref[kind, 0], mats_ref[kind, 1]), data, ((1,), (1,)))

    lane = lax.broadcasted_iota(jnp.int32, (256, 128), 1)
    for half in range(2):
        positive, negative = mixed(POS, 256 * half, 256), mixed(NEG, 512 + 256 * half, 256)
        for pair in range(2):
            at = slice(128 * pair, 128 * pair + 128)
            one, two = positive[:, at], negative[:, at]
            low = (lane & 32) == 0
            even, odd = jnp.where(low, one, two), jnp.where(low, two, one)
            if half == 0 and pair == 0:
                even = jnp.where((lane & 48) == 0, mixed(ZERO, 0, 128), even)
                even = jnp.where((lane & 48) == 32, mixed(HALF, 512, 128), even)
            for side, block in enumerate([even, odd]):
                quad = 4 * half + 2 * pair + side
                out_ref[pl.ds(32 * quad, 32)] = block.reshape(32, 8, 128)


def sine_turns(turns):
    t = turns - jnp.round(turns)
    square = t * t
    total = SINE[-1]
    for coefficient in SINE[-2::-1]:
        total = total * square + coefficient
    return total * t


def sine_fit():
    nodes = np.cos(np.pi * (np.arange(400) + 0.5) / 800) * 0.5
    basis = np.stack([nodes ** (2 * k + 1) for k in range(6)], 1)
    return [float(c) for c in np.linalg.lstsq(basis, np.sin(2 * np.pi * nodes), rcond=None)[0]]


SINE = sine_fit()


def device_number():
    n = 8 * lax.axis_index("row") + lax.axis_index("col")
    return 2 * (n % 128) + n // 128


def arc_tangent(value):
    for _ in range(2):
        value = value / (1.0 + jnp.sqrt(1.0 + value * value))
    square = value * value
    total = 1.0 / 17.0
    for k in range(15, 0, -2):
        total = 1.0 / k - square * total
    return 4.0 * value * total


def columns_kernel(
    fresnel_ref,
    terms_ref,
    field_ref,
    mats_ref,
    ahead_ref,
    behind_ref,
    spin_ref,
    out_ref,
    work_ref,
    back_ref,
):
    device = device_number()
    quad, group = device // 32, device % 32
    sub = lax.broadcasted_iota(jnp.int32, (8, 128), 0)
    lane = lax.broadcasted_iota(jnp.int32, (8, 128), 1)
    first = (sub & 2) == 0
    sign = jnp.where(first, 1.0, -1.0).astype(F32)

    def shift(value, amount, axis):
        return pltpu.roll(value, amount, axis + value.ndim - 2)

    def swap_pairs(value):
        return jnp.where(first, shift(value, 6, 0), shift(value, 2, 0))

    for nb in range(8):
        lines = []
        for na in range(16):
            n = 8 * na + nb
            one, two = field_ref[2 * n], field_ref[2 * n + 1]
            one, two = one + two, one - two
            line = (jnp.where(first, one, shift(two, 2, 0)), jnp.where(first, shift(one, 6, 0), two))
            if n:
                angle = 2.0 * math.pi * n / 256
                line = times(
                    line,
                    jnp.where(first, 1.0, math.cos(angle)).astype(F32),
                    jnp.where(first, 0.0, -math.sin(angle)).astype(F32),
                )
            lines.append(line)
        for ka, line in enumerate(transform(lines, -1)):
            real, imag = turned(line, nb * ka, 128, -1)
            work_ref[0, ka, nb] = real
            work_ref[1, ka, nb] = imag

    slot = ((lane >> 4) & 3) ^ (2 * (quad & 1))
    s = ((sub >> 2) << 1) | (sub & 1)
    positive = 4 * group + s
    base = 2 * group + (s & 1)
    mirrored = jnp.where(s < 2, base, jnp.where(base == 0, 64, 128 - base))
    halfway = jnp.where(s < 2, base, 127 - base)
    k2 = jnp.where(slot < 2, positive, 127 - positive)
    k1 = 2 * quad + (slot & 1)
    k1 = jnp.where(slot < 2, k1, 32 - k1)
    special = (quad == 0) & ((slot & 1) == 0)
    k2 = jnp.where(special, jnp.where(slot == 0, mirrored, halfway), k2)
    k1 = jnp.where(special, jnp.where(slot == 0, 0, 16), k1)
    v = k1 + 32 * k2
    v = jnp.where(v >= N // 2, v - N, v).astype(F32)
    v_square = v * v
    a2 = lane & 15
    u_base = (((sub >> 1) & 1) + 256 * a2 - jnp.where(a2 >= 8, N, 0)).astype(F32)
    later = lane >= 64
    rate_even = (0.5 / (N * N)) / jnp.where(later, fresnel_ref[2], fresnel_ref[0])
    rate_odd = (0.5 / (N * N)) / jnp.where(later, fresnel_ref[3], fresnel_ref[1])
    ratio = jnp.full((8, 128), terms_ref[0], F32)
    offset = arc_tangent(ratio) * (0.5 / math.pi)
    gain = 2.0 * jnp.sqrt(1.0 + ratio * ratio)
    floor = terms_ref[1] / gain

    def rows_of(table, which, start, count, stride):
        picked = []
        for part in range(2):
            tiles = []
            for k in range(count):
                at = pl.ds(start + stride * k, 1)
                upper = jnp.broadcast_to(table[which + (part, 0, at)], (8, 128))
                lower = jnp.broadcast_to(table[which + (part, 1, at)], (8, 128))
                tiles.append(jnp.where(first, upper, lower))
            picked.append(jnp.stack(tiles))
        return picked

    forward = (mats_ref[0], mats_ref[1])
    inverse = (mats_ref[2], mats_ref[3])
    natural = ((1,), (0,))
    for bunch in range(4):
        reals, imags = [], []
        for ka in range(4 * bunch, 4 * bunch + 4):
            lines = transform([(work_ref[0, ka, nb], work_ref[1, ka, nb]) for nb in range(8)], -1)
            real = jnp.stack([z[0] for z in lines])
            imag = jnp.stack([z[1] for z in lines])
            cosine, sine = (
                jnp.stack([ahead_ref[part, ka + 16 * kb] for kb in range(8)]) for part in range(2)
            )
            real, imag = times((real, imag), cosine, -sine)
            reals.append(real.reshape(64, 128))
            imags.append(imag.reshape(64, 128))
        mixed = jnp.concatenate(
            [jnp.concatenate(reals, 0), jnp.concatenate(imags, 0)], 1
        )
        mixed = product(split(mixed), forward, natural)
        reals, imags = [], []
        for step in range(4):
            ka = 4 * bunch + step
            rows = slice(64 * step, 64 * step + 64)
            real = mixed[rows, :128].reshape(8, 8, 128)
            imag = mixed[rows, 128:].reshape(8, 8, 128)
            for kb in range(8):
                u = u_base + float(2 * ka + 32 * kb)
                radius = u * u + v_square
                even = sine_turns(radius * rate_even + offset)
                odd = sine_turns(radius * rate_odd + offset)
                energy = even * even + odd * odd
                scale = 1.0 / (gain * (energy + shift(energy, 64, 1)) + floor)
                reals.append((even * real[kb] + odd * imag[kb]) * scale)
                imags.append((even * imag[kb] - odd * real[kb]) * scale)
        mixed = jnp.concatenate(
            [jnp.concatenate(reals, 0), jnp.concatenate(imags, 0)], 1
        )
        mixed = product(split(mixed), inverse, natural)
        for step in range(4):
            ka = 4 * bunch + step
            rows = slice(64 * step, 64 * step + 64)
            real = mixed[rows, :128].reshape(8, 8, 128)
            imag = mixed[rows, 128:].reshape(8, 8, 128)
            early = times((real[:4], imag[:4]), *rows_of(behind_ref, (0,), ka, 4, 16))
            later_half = times((real[4:], imag[4:]), *rows_of(behind_ref, (1,), ka, 4, 16))
            real, imag = plus(early, later_half)
            back_ref[0, ka] = real
            back_ref[1, ka] = imag

    for wb in range(8):
        lines = [
            tuple(back_ref[part, wb + 8 * (wa % 2), wa // 2] for part in range(2)) for wa in range(8)
        ]
        for na, line in enumerate(transform(lines, 1)):
            real, imag = turned(line, wb * na, 64, 1)
            work_ref[0, na, wb] = real
            work_ref[1, na, wb] = imag
    bit5 = (lane & 32) != 0
    reflected = (quad == 0) & ((lane & 16) == 0)
    itself = (quad == 0) & (group == 0) & ((lane & 48) == 0) & ((sub & 1) == 0)
    low_half = (lane & 8) == 0
    straight = ((sub & 4) != 0) == (lane >= 64)

    def partner(value):
        across = jnp.where(bit5, shift(value, 32, 1), shift(value, 96, 1))
        down = jnp.where(itself, value, shift(value, 4, 0))
        return jnp.where(reflected, down, across)

    for na in range(8):
        lines = [(work_ref[0, na, wb], work_ref[1, na, wb]) for wb in range(8)]
        for nb, line in enumerate(transform(lines, 1)):
            at = pl.ds(na + 8 * nb, 1)
            cosine, sine = (jnp.broadcast_to(spin_ref[part, at], (8, 128)) for part in range(2))
            line = times(line, jnp.where(first, 1.0, cosine), jnp.where(first, 0.0, sine))
            real, imag = (swap_pairs(z) + sign * z for z in line)
            real, imag = real + partner(real), imag - partner(imag)
            packed = real + jnp.where(low_half, -shift(imag, 120, 1), shift(imag, 8, 1))
            crossed = shift(shift(packed, 64, 1), 4, 0)
            out_ref[na + 8 * nb] = jnp.where(straight, packed, crossed)


def image_kernel(field_ref, mats_ref, twist_ref, out_ref):
    lane = lax.broadcasted_iota(jnp.int32, (64, 128), 1)
    bit6, bit3 = (lane & 64) != 0, (lane & 8) != 0
    tiles = {}
    for half in range(2):
        quads = [field_ref[pl.ds(256 * half + 64 * q, 64), :] for q in range(4)]
        parts = []
        for qb in range(2):
            one, two = quads[qb], quads[2 + qb]
            parts.append(
                (
                    jnp.where(bit6, pltpu.roll(two, 64, 1), one),
                    jnp.where(bit6, two, pltpu.roll(one, 64, 1)),
                )
            )
        stacked = []
        for s1 in range(2):
            one, two = parts[0][s1], parts[1][s1]
            stacked.append(jnp.where(bit3, pltpu.roll(two, 8, 1), one))
            stacked.append(jnp.where(bit3, two, pltpu.roll(one, 120, 1)))
        lines = jnp.concatenate(stacked, 0).T
        for q in range(4):
            for slot, k1 in enumerate(residues(4 * half + q)):
                start = 64 * (q // 2) + 16 * slot + 8 * (q % 2)
                tiles[k1] = lines[start : start + 8]
    lines = {}
    for kind, members in (
        (POS, [1, *range(1, 16)]),
        (NEG, [17, *range(17, 32)]),
        (ZERO, [0, 0]),
        (HALF, [16, 16]),
    ):
        data = split(jnp.concatenate([tiles[k1] for k1 in members], 0))
        value = product(data, (mats_ref[kind, 0], mats_ref[kind, 1]), ((1,), (0,)))
        for k, k1 in enumerate(members):
            line = (value[8 * k : 8 * k + 8, :128], value[8 * k : 8 * k + 8, 128:])
            lines[k1] = times(line, twist_ref[0, pl.ds(k1, 1), :], twist_ref[1, pl.ds(k1, 1), :])
    for n1, (real, imag) in enumerate(transform([lines[k1] for k1 in range(32)], 1)):
        at = pl.ds(128 * (n1 % 4), 128)
        out_ref[n1 // 4, pl.ds(0, 8), at] = real
        out_ref[n1 // 4, pl.ds(8, 8), at] = imag


def call(kernel, out_shape, scratch, arguments, spaces):
    return pl.pallas_call(
        kernel,
        out_shape=jax.ShapeDtypeStruct(out_shape, F32),
        in_specs=[pl.BlockSpec(memory_space=space) for space in spaces],
        out_specs=pl.BlockSpec(memory_space=pltpu.VMEM),
        scratch_shapes=scratch,
        compiler_params=pltpu.CompilerParams(vmem_limit_bytes=40 * 1024 * 1024),
    )(*arguments)


def image_rows(field):
    arguments = [field] + [jnp.asarray(c) for c in row_constants()]
    scratch = [pltpu.VMEM((1024, 256), BF16), pltpu.VMEM((1024, 256), BF16)]
    return call(rows_kernel, (256, 8, 128), scratch, arguments, [pltpu.VMEM] * 3)


def filter_columns(field, fresnel, ctf_terms):
    constants = [jnp.asarray(c) for c in column_constants()]
    scratch = [pltpu.VMEM((2, 16, 8, 8, 128), F32), pltpu.VMEM((2, 16, 4, 8, 128), F32)]
    spaces = [pltpu.SMEM] * 2 + [pltpu.VMEM] * 5
    arguments = [fresnel, ctf_terms, field] + constants
    return call(columns_kernel, (64, 8, 128), scratch, arguments, spaces)


def image_from(field):
    arguments = [field] + [jnp.asarray(c) for c in image_constants()]
    return call(image_kernel, (8, 16, 512), [], arguments, [pltpu.VMEM] * 3)


STEPS = [(2, 1), (0, 1), (2, 0), (1, 1), (3, 0), (3, 1), (1, 0)]


def ring_exchange(field):
    me = lax.axis_index("col")
    own = lax.dynamic_slice_in_dim(field, me, 1, 1)
    result = jnp.zeros((8, 4, 16, 512), F32)
    result = lax.dynamic_update_slice_in_dim(result, own.transpose(1, 0, 2, 3), me, 0)
    for step, flip in STEPS:

        def there(place, sign):
            return (place // 4 ^ flip) * 4 + (place + sign * step) % 4

        chunk = lax.dynamic_slice_in_dim(field, there(me, 1), 1, 1)
        pairs = [(place, there(place, 1)) for place in range(8)]
        chunk = lax.ppermute(chunk.reshape(1, 4, 16, 512), "col", pairs)
        result = lax.dynamic_update_slice_in_dim(result, chunk, there(me, -1), 0)
    return result


def exchange(field):
    return lax.all_to_all(field, "col", split_axis=0, concat_axis=0, tiled=True)


def exchange_all(field):
    return lax.all_to_all(
        field, ("row", "col"), split_axis=0, concat_axis=0, tiled=True, axis_index_groups=[ORDER]
    )


def local(holograms, fresnel, ctf_terms):
    field = image_rows(ring_exchange(holograms.reshape(4, 8, 16, 512)))
    field = filter_columns(exchange_all(field), fresnel, ctf_terms)
    field = exchange_all(field.reshape(256, 2, 128))
    image = image_from(field.reshape(512, 128))
    return exchange(image).reshape(128, 512)


def solution(mesh):
    in_specs = (P(None, "row", "col"), P(), P())
    out_specs = P("row", "col")
    return jax.shard_map(local, mesh=mesh, in_specs=in_specs, out_specs=out_specs, check_vma=False)
```

```python
import math

import jax
import jax.numpy as jnp
import ml_dtypes
import numpy as np
from jax import lax
from jax.experimental import pallas as pl
from jax.experimental.pallas import tpu as pltpu
from jax.sharding import PartitionSpec as P

N = 4096
POS, NEG, ZERO, HALF = range(4)
ORDER = [128 * (place % 2) + place // 2 for place in range(256)]
F32 = jnp.float32
BF16 = jnp.bfloat16


def residues(quad):
    low, high = 2 * quad, 2 * quad + 1
    if quad == 0:
        return [0, 1, 16, 31]
    if quad % 2:
        return [32 - low, 32 - high, low, high]
    return [low, high, 32 - low, 32 - high]


def member(kind, group, slot):
    if kind == POS:
        return 4 * group + slot
    if kind == NEG:
        return 127 - 4 * group - slot
    if kind == ZERO:
        return [2 * group, 2 * group + 1, 128 - 2 * group if group else 64, 127 - 2 * group][slot]
    return [2 * group, 2 * group + 1, 127 - 2 * group, 126 - 2 * group][slot]


def halves(matrix):
    high = matrix.astype(ml_dtypes.bfloat16)
    low = (matrix - high.astype(np.float64)).astype(ml_dtypes.bfloat16)
    return np.stack([high, low])


def turn(product, length):
    angle = 2.0 * np.pi * (np.asarray(product, np.int64) % length) / length
    return np.cos(angle), np.sin(angle)


def line_twist():
    return np.stack(turn(np.arange(32)[:, None] * np.arange(128), N)).astype(np.float32)


def row_constants():
    mats = []
    for kind in range(4):
        k2 = np.array([[member(kind, g, s) for s in range(4)] for g in range(32)])
        cosine, sine = turn(k2[:, :, None] * np.arange(128), 128)
        real = np.concatenate([cosine, sine], -1)
        imag = np.concatenate([-sine, cosine], -1)
        both = np.stack([real.reshape(32, 2, 2, 256), imag.reshape(32, 2, 2, 256)], 2)
        mats.append(halves(both.reshape(256, 256)))
    return np.stack(mats), line_twist()


def column_constants():
    cosine, sine = turn(np.arange(16)[:, None] * np.arange(16), 16)
    eye8 = np.eye(8)
    forward = np.block(
        [
            [np.kron(eye8, cosine), np.kron(eye8, -sine)],
            [np.kron(eye8, sine), np.kron(eye8, cosine)],
        ]
    )
    pick = np.kron(np.ones((2, 2)), np.eye(4))

    def spread(block):
        return np.kron(pick, block)

    inverse = np.block([[spread(cosine), spread(sine)], [spread(-sine), spread(cosine)]])
    lane = np.arange(128)
    within = lane % 16
    top = lane // 64
    parity = np.arange(2)[:, None, None]
    ahead = np.stack(turn((2 * np.arange(128)[None, :, None] + parity) * within, N))
    steps = np.arange(64)[None, :, None]
    behind = [
        turn((2 * steps + parity + 128 * h) * within + (32 * steps + 2048 * h) * top, N)
        for h in range(2)
    ]
    spin = np.stack(turn(2 * np.arange(64)[:, None] + top, 256)).astype(np.float32)
    ahead = np.repeat(ahead[:, [0, 1, 0, 1]].transpose(0, 2, 1, 3), 2, 2)
    ahead, behind = ahead.astype(np.float32), np.stack(behind).astype(np.float32)
    return np.concatenate([halves(forward), halves(inverse)]), ahead, behind, spin


def image_constants():
    mats = []
    for kind in range(4):
        k2 = np.array([[member(kind, g, s) for g in range(32)] for s in range(4)])
        k2 = k2.reshape(2, 2, 32).transpose(0, 2, 1).reshape(2, 64)
        cosine, sine = turn(k2[:, :, None] * np.arange(128), 128)
        real = np.concatenate([cosine, sine], -1)
        imag = np.concatenate([-sine, cosine], -1)
        mats.append(halves(np.stack([real, imag], 1).reshape(256, 256) * (0.5 / (N * N))))
    return np.stack(mats), line_twist()


def turned(value, angle_index, length, sign):
    angle_index %= length
    real, imag = value
    if angle_index == 0:
        return value
    if 4 * angle_index == length:
        return (-imag, real) if sign > 0 else (imag, -real)
    if 2 * angle_index == length:
        return (-real, -imag)
    if 4 * angle_index == 3 * length:
        return (imag, -real) if sign > 0 else (-imag, real)
    angle = sign * 2.0 * math.pi * angle_index / length
    cosine, sine = math.cos(angle), math.sin(angle)
    if (8 * angle_index) % length == 0:
        scale = abs(cosine)
        plus, minus = (real + imag) * scale, (real - imag) * scale
        if cosine > 0:
            return (minus, plus) if sine > 0 else (plus, -minus)
        return (-plus, minus) if sine > 0 else (-minus, -plus)
    return (real * cosine - imag * sine, imag * cosine + real * sine)


def plus(a, b):
    return (a[0] + b[0], a[1] + b[1])


def minus(a, b):
    return (a[0] - b[0], a[1] - b[1])


def transform(values, sign):
    length = len(values)
    if length == 1:
        return values
    if length == 2:
        return [plus(values[0], values[1]), minus(values[0], values[1])]
    quarter = length // 4
    columns = []
    for b in range(quarter):
        z0, z1, z2, z3 = (values[a * quarter + b] for a in range(4))
        even, odd = plus(z0, z2), plus(z1, z3)
        even_gap, odd_gap = minus(z0, z2), turned(minus(z1, z3), 1, 4, sign)
        outs = [plus(even, odd), plus(even_gap, odd_gap), minus(even, odd), minus(even_gap, odd_gap)]
        columns.append([turned(z, b * k, length, sign) for k, z in enumerate(outs)])
    result = [None] * length
    for k in range(4):
        for m, z in enumerate(transform([columns[b][k] for b in range(quarter)], sign)):
            result[k + 4 * m] = z
    return result


def times(value, cosine, sine):
    real, imag = value
    return (real * cosine - imag * sine, imag * cosine + real * sine)


def split(value):
    high = value.astype(BF16)
    return high, (value - high.astype(F32)).astype(BF16)


def product(left, right, dims):
    def one(a, b):
        return lax.dot_general(a, b, (dims, ((), ())), preferred_element_type=F32)

    return one(left[0], right[0]) + (one(left[0], right[1]) + one(left[1], right[0]))


def rows_kernel(field_ref, mats_ref, twist_ref, out_ref, high_ref, low_ref):
    for j in range(2):
        lines = []
        for n1 in range(32):
            at = pl.ds(128 * (n1 % 4), 128)
            lines.append(
                (field_ref[n1 // 4, 2 * j, :, at], field_ref[n1 // 4, 2 * j + 1, :, at])
            )
        lines = transform(lines, -1)
        for k1, line in enumerate(lines):
            if k1:
                line = times(line, twist_ref[0, pl.ds(k1, 1), :], -twist_ref[1, pl.ds(k1, 1), :])
            place = k1 if k1 < 16 else 16 + ((32 - k1) % 16 ^ 2)
            rows = pl.ds(128 * (place // 4) + 64 * j + 16 * (place % 4), 16)
            for part in range(2):
                high, low = split(line[part])
                high_ref[rows, pl.ds(128 * part, 128)] = high
                low_ref[rows, pl.ds(128 * part, 128)] = low

    def mixed(kind, start, count):
        rows = pl.ds(start, count)
        data = (high_ref[rows, :], low_ref[rows, :])
        return product((mats_ref[kind, 0], mats_ref[kind, 1]), data, ((1,), (1,)))

    lane = lax.broadcasted_iota(jnp.int32, (256, 128), 1)
    for half in range(2):
        positive, negative = mixed(POS, 256 * half, 256), mixed(NEG, 512 + 256 * half, 256)
        for pair in range(2):
            at = slice(128 * pair, 128 * pair + 128)
            one, two = positive[:, at], negative[:, at]
            low = (lane & 32) == 0
            even, odd = jnp.where(low, one, two), jnp.where(low, two, one)
            if half == 0 and pair == 0:
                even = jnp.where((lane & 48) == 0, mixed(ZERO, 0, 128), even)
                even = jnp.where((lane & 48) == 32, mixed(HALF, 512, 128), even)
            for side, block in enumerate([even, odd]):
                quad = 4 * half + 2 * pair + side
                out_ref[pl.ds(32 * quad, 32)] = block.reshape(32, 8, 128)


def sine_turns(turns):
    t = turns - jnp.round(turns)
    square = t * t
    total = SINE[-1]
    for coefficient in SINE[-2::-1]:
        total = total * square + coefficient
    return total * t


def sine_fit():
    nodes = np.cos(np.pi * (np.arange(400) + 0.5) / 800) * 0.5
    basis = np.stack([nodes ** (2 * k + 1) for k in range(6)], 1)
    return [float(c) for c in np.linalg.lstsq(basis, np.sin(2 * np.pi * nodes), rcond=None)[0]]


SINE = sine_fit()


def device_number():
    n = 8 * lax.axis_index("row") + lax.axis_index("col")
    return 2 * (n % 128) + n // 128


def arc_tangent(value):
    for _ in range(2):
        value = value / (1.0 + jnp.sqrt(1.0 + value * value))
    square = value * value
    total = 1.0 / 17.0
    for k in range(15, 0, -2):
        total = 1.0 / k - square * total
    return 4.0 * value * total


def columns_kernel(
    fresnel_ref,
    terms_ref,
    field_ref,
    mats_ref,
    ahead_ref,
    behind_ref,
    spin_ref,
    out_ref,
    work_ref,
    back_ref,
):
    device = device_number()
    quad, group = device // 32, device % 32
    sub = lax.broadcasted_iota(jnp.int32, (8, 128), 0)
    lane = lax.broadcasted_iota(jnp.int32, (8, 128), 1)
    first = (sub & 2) == 0
    sign = jnp.where(first, 1.0, -1.0).astype(F32)

    def shift(value, amount, axis):
        return pltpu.roll(value, amount, axis + value.ndim - 2)

    def swap_pairs(value):
        return jnp.where(first, shift(value, 6, 0), shift(value, 2, 0))

    for nb in range(8):
        lines = []
        for na in range(16):
            n = 8 * na + nb
            one, two = field_ref[2 * n], field_ref[2 * n + 1]
            one, two = one + two, one - two
            line = (jnp.where(first, one, shift(two, 2, 0)), jnp.where(first, shift(one, 6, 0), two))
            if n:
                angle = 2.0 * math.pi * n / 256
                line = times(
                    line,
                    jnp.where(first, 1.0, math.cos(angle)).astype(F32),
                    jnp.where(first, 0.0, -math.sin(angle)).astype(F32),
                )
            lines.append(line)
        for ka, line in enumerate(transform(lines, -1)):
            real, imag = turned(line, nb * ka, 128, -1)
            work_ref[0, ka, nb] = real
            work_ref[1, ka, nb] = imag

    slot = ((lane >> 4) & 3) ^ (2 * (quad & 1))
    s = ((sub >> 2) << 1) | (sub & 1)
    positive = 4 * group + s
    base = 2 * group + (s & 1)
    mirrored = jnp.where(s < 2, base, jnp.where(base == 0, 64, 128 - base))
    halfway = jnp.where(s < 2, base, 127 - base)
    k2 = jnp.where(slot < 2, positive, 127 - positive)
    k1 = 2 * quad + (slot & 1)
    k1 = jnp.where(slot < 2, k1, 32 - k1)
    special = (quad == 0) & ((slot & 1) == 0)
    k2 = jnp.where(special, jnp.where(slot == 0, mirrored, halfway), k2)
    k1 = jnp.where(special, jnp.where(slot == 0, 0, 16), k1)
    v = k1 + 32 * k2
    v = jnp.where(v >= N // 2, v - N, v).astype(F32)
    v_square = v * v
    a2 = lane & 15
    u_base = (((sub >> 1) & 1) + 256 * a2 - jnp.where(a2 >= 8, N, 0)).astype(F32)
    later = lane >= 64
    rate_even = (0.5 / (N * N)) / jnp.where(later, fresnel_ref[2], fresnel_ref[0])
    rate_odd = (0.5 / (N * N)) / jnp.where(later, fresnel_ref[3], fresnel_ref[1])
    ratio = jnp.full((8, 128), terms_ref[0], F32)
    offset = arc_tangent(ratio) * (0.5 / math.pi)
    gain = 2.0 * jnp.sqrt(1.0 + ratio * ratio)
    floor = terms_ref[1] / gain

    def rows_of(table, which, start, count, stride):
        picked = []
        for part in range(2):
            tiles = []
            for k in range(count):
                at = pl.ds(start + stride * k, 1)
                upper = jnp.broadcast_to(table[which + (part, 0, at)], (8, 128))
                lower = jnp.broadcast_to(table[which + (part, 1, at)], (8, 128))
                tiles.append(jnp.where(first, upper, lower))
            picked.append(jnp.stack(tiles))
        return picked

    forward = (mats_ref[0], mats_ref[1])
    inverse = (mats_ref[2], mats_ref[3])
    natural = ((1,), (0,))
    for bunch in range(4):
        reals, imags = [], []
        for ka in range(4 * bunch, 4 * bunch + 4):
            lines = transform([(work_ref[0, ka, nb], work_ref[1, ka, nb]) for nb in range(8)], -1)
            real = jnp.stack([z[0] for z in lines])
            imag = jnp.stack([z[1] for z in lines])
            cosine, sine = (
                jnp.stack([ahead_ref[part, ka + 16 * kb] for kb in range(8)]) for part in range(2)
            )
            real, imag = times((real, imag), cosine, -sine)
            reals.append(real.reshape(64, 128))
            imags.append(imag.reshape(64, 128))
        mixed = jnp.concatenate(
            [jnp.concatenate(reals, 0), jnp.concatenate(imags, 0)], 1
        )
        mixed = product(split(mixed), forward, natural)
        reals, imags = [], []
        for step in range(4):
            ka = 4 * bunch + step
            rows = slice(64 * step, 64 * step + 64)
            real = mixed[rows, :128].reshape(8, 8, 128)
            imag = mixed[rows, 128:].reshape(8, 8, 128)
            for kb in range(8):
                u = u_base + float(2 * ka + 32 * kb)
                radius = u * u + v_square
                even = sine_turns(radius * rate_even + offset)
                odd = sine_turns(radius * rate_odd + offset)
                energy = even * even + odd * odd
                scale = 1.0 / (gain * (energy + shift(energy, 64, 1)) + floor)
                reals.append((even * real[kb] + odd * imag[kb]) * scale)
                imags.append((even * imag[kb] - odd * real[kb]) * scale)
        mixed = jnp.concatenate(
            [jnp.concatenate(reals, 0), jnp.concatenate(imags, 0)], 1
        )
        mixed = product(split(mixed), inverse, natural)
        for step in range(4):
            ka = 4 * bunch + step
            rows = slice(64 * step, 64 * step + 64)
            real = mixed[rows, :128].reshape(8, 8, 128)
            imag = mixed[rows, 128:].reshape(8, 8, 128)
            early = times((real[:4], imag[:4]), *rows_of(behind_ref, (0,), ka, 4, 16))
            later_half = times((real[4:], imag[4:]), *rows_of(behind_ref, (1,), ka, 4, 16))
            real, imag = plus(early, later_half)
            back_ref[0, ka] = real
            back_ref[1, ka] = imag

    for wb in range(8):
        lines = [
            tuple(back_ref[part, wb + 8 * (wa % 2), wa // 2] for part in range(2)) for wa in range(8)
        ]
        for na, line in enumerate(transform(lines, 1)):
            real, imag = turned(line, wb * na, 64, 1)
            work_ref[0, na, wb] = real
            work_ref[1, na, wb] = imag
    bit5 = (lane & 32) != 0
    reflected = (quad == 0) & ((lane & 16) == 0)
    itself = (quad == 0) & (group == 0) & ((lane & 48) == 0) & ((sub & 1) == 0)
    low_half = (lane & 8) == 0
    straight = ((sub & 4) != 0) == (lane >= 64)

    def partner(value):
        across = jnp.where(bit5, shift(value, 32, 1), shift(value, 96, 1))
        down = jnp.where(itself, value, shift(value, 4, 0))
        return jnp.where(reflected, down, across)

    for na in range(8):
        lines = [(work_ref[0, na, wb], work_ref[1, na, wb]) for wb in range(8)]
        for nb, line in enumerate(transform(lines, 1)):
            at = pl.ds(na + 8 * nb, 1)
            cosine, sine = (jnp.broadcast_to(spin_ref[part, at], (8, 128)) for part in range(2))
            line = times(line, jnp.where(first, 1.0, cosine), jnp.where(first, 0.0, sine))
            real, imag = (swap_pairs(z) + sign * z for z in line)
            real, imag = real + partner(real), imag - partner(imag)
            packed = real + jnp.where(low_half, -shift(imag, 120, 1), shift(imag, 8, 1))
            crossed = shift(shift(packed, 64, 1), 4, 0)
            out_ref[na + 8 * nb] = jnp.where(straight, packed, crossed)


def image_kernel(field_ref, mats_ref, twist_ref, out_ref):
    lane = lax.broadcasted_iota(jnp.int32, (64, 128), 1)
    bit6, bit3 = (lane & 64) != 0, (lane & 8) != 0
    tiles = {}
    for half in range(2):
        quads = [field_ref[pl.ds(256 * half + 64 * q, 64), :] for q in range(4)]
        parts = []
        for qb in range(2):
            one, two = quads[qb], quads[2 + qb]
            parts.append(
                (
                    jnp.where(bit6, pltpu.roll(two, 64, 1), one),
                    jnp.where(bit6, two, pltpu.roll(one, 64, 1)),
                )
            )
        stacked = []
        for s1 in range(2):
            one, two = parts[0][s1], parts[1][s1]
            stacked.append(jnp.where(bit3, pltpu.roll(two, 8, 1), one))
            stacked.append(jnp.where(bit3, two, pltpu.roll(one, 120, 1)))
        lines = jnp.concatenate(stacked, 0).T
        for q in range(4):
            for slot, k1 in enumerate(residues(4 * half + q)):
                start = 64 * (q // 2) + 16 * slot + 8 * (q % 2)
                tiles[k1] = lines[start : start + 8]
    lines = {}
    for kind, members in (
        (POS, [1, *range(1, 16)]),
        (NEG, [17, *range(17, 32)]),
        (ZERO, [0, 0]),
        (HALF, [16, 16]),
    ):
        data = split(jnp.concatenate([tiles[k1] for k1 in members], 0))
        value = product(data, (mats_ref[kind, 0], mats_ref[kind, 1]), ((1,), (0,)))
        for k, k1 in enumerate(members):
            line = (value[8 * k : 8 * k + 8, :128], value[8 * k : 8 * k + 8, 128:])
            lines[k1] = times(line, twist_ref[0, pl.ds(k1, 1), :], twist_ref[1, pl.ds(k1, 1), :])
    for n1, (real, imag) in enumerate(transform([lines[k1] for k1 in range(32)], 1)):
        at = pl.ds(128 * (n1 % 4), 128)
        out_ref[n1 // 4, pl.ds(0, 8), at] = real
        out_ref[n1 // 4, pl.ds(8, 8), at] = imag


def call(kernel, out_shape, scratch, arguments, spaces):
    return pl.pallas_call(
        kernel,
        out_shape=jax.ShapeDtypeStruct(out_shape, F32),
        in_specs=[pl.BlockSpec(memory_space=space) for space in spaces],
        out_specs=pl.BlockSpec(memory_space=pltpu.VMEM),
        scratch_shapes=scratch,
        compiler_params=pltpu.CompilerParams(vmem_limit_bytes=40 * 1024 * 1024),
    )(*arguments)


def image_rows(field):
    arguments = [field] + [jnp.asarray(c) for c in row_constants()]
    scratch = [pltpu.VMEM((1024, 256), BF16), pltpu.VMEM((1024, 256), BF16)]
    return call(rows_kernel, (256, 8, 128), scratch, arguments, [pltpu.VMEM] * 3)


def filter_columns(field, fresnel, ctf_terms):
    constants = [jnp.asarray(c) for c in column_constants()]
    scratch = [pltpu.VMEM((2, 16, 8, 8, 128), F32), pltpu.VMEM((2, 16, 4, 8, 128), F32)]
    spaces = [pltpu.SMEM] * 2 + [pltpu.VMEM] * 5
    arguments = [fresnel, ctf_terms, field] + constants
    return call(columns_kernel, (64, 8, 128), scratch, arguments, spaces)


def image_from(field):
    arguments = [field] + [jnp.asarray(c) for c in image_constants()]
    return call(image_kernel, (8, 16, 512), [], arguments, [pltpu.VMEM] * 3)


STEPS = [(2, 1), (0, 1), (2, 0), (1, 1), (3, 0), (3, 1), (1, 0)]


def ring_exchange(field):
    me = lax.axis_index("col")
    result = jnp.zeros((8, 4, 16, 512), F32)
    for step, flip in STEPS:

        def there(place, sign):
            return (place // 4 ^ flip) * 4 + (place + sign * step) % 4

        chunk = lax.dynamic_slice_in_dim(field, there(me, 1), 1, 1)
        pairs = [(place, there(place, 1)) for place in range(8)]
        chunk = lax.ppermute(chunk.reshape(1, 4, 16, 512), "col", pairs)
        result = lax.dynamic_update_slice_in_dim(result, chunk, there(me, -1), 0)
        if (step, flip) == STEPS[2]:
            own = lax.dynamic_slice_in_dim(field, me, 1, 1)
            result = lax.dynamic_update_slice_in_dim(result, own.transpose(1, 0, 2, 3), me, 0)
    return result


def exchange(field):
    return lax.all_to_all(field, "col", split_axis=0, concat_axis=0, tiled=True)


def exchange_all(field):
    return lax.all_to_all(
        field, ("row", "col"), split_axis=0, concat_axis=0, tiled=True, axis_index_groups=[ORDER]
    )


def local(holograms, fresnel, ctf_terms):
    field = image_rows(ring_exchange(holograms.reshape(4, 8, 16, 512)))
    field = filter_columns(exchange_all(field), fresnel, ctf_terms)
    field = exchange_all(field.reshape(256, 2, 128))
    image = image_from(field.reshape(512, 128))
    return exchange(image).reshape(128, 512)


def solution(mesh):
    in_specs = (P(None, "row", "col"), P(), P())
    out_specs = P("row", "col")
    return jax.shard_map(local, mesh=mesh, in_specs=in_specs, out_specs=out_specs, check_vma=False)
```

```python
import math

import jax
import jax.numpy as jnp
import ml_dtypes
import numpy as np
from jax import lax
from jax.experimental import pallas as pl
from jax.experimental.pallas import tpu as pltpu
from jax.sharding import PartitionSpec as P

N = 4096
POS, NEG, ZERO, HALF = range(4)
ORDER = [128 * (place % 2) + place // 2 for place in range(256)]
F32 = jnp.float32
BF16 = jnp.bfloat16


def residues(quad):
    low, high = 2 * quad, 2 * quad + 1
    if quad == 0:
        return [0, 1, 16, 31]
    if quad % 2:
        return [32 - low, 32 - high, low, high]
    return [low, high, 32 - low, 32 - high]


def member(kind, group, slot):
    if kind == POS:
        return 4 * group + slot
    if kind == NEG:
        return 127 - 4 * group - slot
    if kind == ZERO:
        return [2 * group, 2 * group + 1, 128 - 2 * group if group else 64, 127 - 2 * group][slot]
    return [2 * group, 2 * group + 1, 127 - 2 * group, 126 - 2 * group][slot]


def halves(matrix):
    high = matrix.astype(ml_dtypes.bfloat16)
    low = (matrix - high.astype(np.float64)).astype(ml_dtypes.bfloat16)
    return np.stack([high, low])


def turn(product, length):
    angle = 2.0 * np.pi * (np.asarray(product, np.int64) % length) / length
    return np.cos(angle), np.sin(angle)


def line_twist():
    return np.stack(turn(np.arange(32)[:, None] * np.arange(128), N)).astype(np.float32)


def row_constants():
    mats = []
    for kind in range(4):
        k2 = np.array([[member(kind, g, s) for s in range(4)] for g in range(32)])
        cosine, sine = turn(k2[:, :, None] * np.arange(128), 128)
        real = np.concatenate([cosine, sine], -1)
        imag = np.concatenate([-sine, cosine], -1)
        both = np.stack([real.reshape(32, 2, 2, 256), imag.reshape(32, 2, 2, 256)], 2)
        mats.append(halves(both.reshape(256, 256)))
    return np.stack(mats), line_twist()


def column_constants():
    cosine, sine = turn(np.arange(16)[:, None] * np.arange(16), 16)
    eye8 = np.eye(8)
    forward = np.block(
        [
            [np.kron(eye8, cosine), np.kron(eye8, -sine)],
            [np.kron(eye8, sine), np.kron(eye8, cosine)],
        ]
    )
    pick = np.kron(np.ones((2, 2)), np.eye(4))

    def spread(block):
        return np.kron(pick, block)

    inverse = np.block([[spread(cosine), spread(sine)], [spread(-sine), spread(cosine)]])
    lane = np.arange(128)
    within = lane % 16
    top = lane // 64
    parity = np.arange(2)[:, None, None]
    ahead = np.stack(turn((2 * np.arange(128)[None, :, None] + parity) * within, N))
    steps = np.arange(64)[None, :, None]
    behind = [
        turn((2 * steps + parity + 128 * h) * within + (32 * steps + 2048 * h) * top, N)
        for h in range(2)
    ]
    spin = np.stack(turn(2 * np.arange(64)[:, None] + top, 256)).astype(np.float32)
    ahead = np.repeat(ahead[:, [0, 1, 0, 1]].transpose(0, 2, 1, 3), 2, 2)
    ahead, behind = ahead.astype(np.float32), np.stack(behind).astype(np.float32)
    return np.concatenate([halves(forward), halves(inverse)]), ahead, behind, spin


def image_constants():
    mats = []
    for kind in range(4):
        k2 = np.array([[member(kind, g, s) for g in range(32)] for s in range(4)])
        k2 = k2.reshape(2, 2, 32).transpose(0, 2, 1).reshape(2, 64)
        cosine, sine = turn(k2[:, :, None] * np.arange(128), 128)
        real = np.concatenate([cosine, sine], -1)
        imag = np.concatenate([-sine, cosine], -1)
        mats.append(halves(np.stack([real, imag], 1).reshape(256, 256) * (0.5 / (N * N))))
    return np.stack(mats), line_twist()


def turned(value, angle_index, length, sign):
    angle_index %= length
    real, imag = value
    if angle_index == 0:
        return value
    if 4 * angle_index == length:
        return (-imag, real) if sign > 0 else (imag, -real)
    if 2 * angle_index == length:
        return (-real, -imag)
    if 4 * angle_index == 3 * length:
        return (imag, -real) if sign > 0 else (-imag, real)
    angle = sign * 2.0 * math.pi * angle_index / length
    cosine, sine = math.cos(angle), math.sin(angle)
    if (8 * angle_index) % length == 0:
        scale = abs(cosine)
        plus, minus = (real + imag) * scale, (real - imag) * scale
        if cosine > 0:
            return (minus, plus) if sine > 0 else (plus, -minus)
        return (-plus, minus) if sine > 0 else (-minus, -plus)
    return (real * cosine - imag * sine, imag * cosine + real * sine)


def plus(a, b):
    return (a[0] + b[0], a[1] + b[1])


def minus(a, b):
    return (a[0] - b[0], a[1] - b[1])


def transform(values, sign):
    length = len(values)
    if length == 1:
        return values
    if length == 2:
        return [plus(values[0], values[1]), minus(values[0], values[1])]
    quarter = length // 4
    columns = []
    for b in range(quarter):
        z0, z1, z2, z3 = (values[a * quarter + b] for a in range(4))
        even, odd = plus(z0, z2), plus(z1, z3)
        even_gap, odd_gap = minus(z0, z2), turned(minus(z1, z3), 1, 4, sign)
        outs = [plus(even, odd), plus(even_gap, odd_gap), minus(even, odd), minus(even_gap, odd_gap)]
        columns.append([turned(z, b * k, length, sign) for k, z in enumerate(outs)])
    result = [None] * length
    for k in range(4):
        for m, z in enumerate(transform([columns[b][k] for b in range(quarter)], sign)):
            result[k + 4 * m] = z
    return result


def times(value, cosine, sine):
    real, imag = value
    return (real * cosine - imag * sine, imag * cosine + real * sine)


def split(value):
    high = value.astype(BF16)
    return high, (value - high.astype(F32)).astype(BF16)


def product(left, right, dims):
    def one(a, b):
        return lax.dot_general(a, b, (dims, ((), ())), preferred_element_type=F32)

    return one(left[0], right[0]) + (one(left[0], right[1]) + one(left[1], right[0]))


def rows_kernel(*refs):
    chunk_refs = refs[:8]
    mats_ref, twist_ref, out_ref, high_ref, low_ref, field_ref = refs[8:]
    me = column_number()
    for (step, flip), chunk_ref in zip(STEPS + [(0, 0)], chunk_refs):
        field_ref[there(me, -step, flip)] = chunk_ref[...]
    for j in range(2):
        lines = []
        for n1 in range(32):
            at = pl.ds(128 * (n1 % 4), 128)
            lines.append(
                (field_ref[n1 // 4, 2 * j, :, at], field_ref[n1 // 4, 2 * j + 1, :, at])
            )
        lines = transform(lines, -1)
        for k1, line in enumerate(lines):
            if k1:
                line = times(line, twist_ref[0, pl.ds(k1, 1), :], -twist_ref[1, pl.ds(k1, 1), :])
            place = k1 if k1 < 16 else 16 + ((32 - k1) % 16 ^ 2)
            rows = pl.ds(128 * (place // 4) + 64 * j + 16 * (place % 4), 16)
            for part in range(2):
                high, low = split(line[part])
                high_ref[rows, pl.ds(128 * part, 128)] = high
                low_ref[rows, pl.ds(128 * part, 128)] = low

    def mixed(kind, start, count):
        rows = pl.ds(start, count)
        data = (high_ref[rows, :], low_ref[rows, :])
        return product((mats_ref[kind, 0], mats_ref[kind, 1]), data, ((1,), (1,)))

    lane = lax.broadcasted_iota(jnp.int32, (256, 128), 1)
    for half in range(2):
        positive, negative = mixed(POS, 256 * half, 256), mixed(NEG, 512 + 256 * half, 256)
        for pair in range(2):
            at = slice(128 * pair, 128 * pair + 128)
            one, two = positive[:, at], negative[:, at]
            low = (lane & 32) == 0
            even, odd = jnp.where(low, one, two), jnp.where(low, two, one)
            if half == 0 and pair == 0:
                even = jnp.where((lane & 48) == 0, mixed(ZERO, 0, 128), even)
                even = jnp.where((lane & 48) == 32, mixed(HALF, 512, 128), even)
            for side, block in enumerate([even, odd]):
                quad = 4 * half + 2 * pair + side
                out_ref[pl.ds(32 * quad, 32)] = block.reshape(32, 8, 128)


def sine_turns(turns):
    t = turns - jnp.round(turns)
    square = t * t
    total = SINE[-1]
    for coefficient in SINE[-2::-1]:
        total = total * square + coefficient
    return total * t


def sine_fit():
    nodes = np.cos(np.pi * (np.arange(400) + 0.5) / 800) * 0.5
    basis = np.stack([nodes ** (2 * k + 1) for k in range(6)], 1)
    return [float(c) for c in np.linalg.lstsq(basis, np.sin(2 * np.pi * nodes), rcond=None)[0]]


SINE = sine_fit()


def column_number():
    return lax.axis_index("col")


def device_number():
    n = 8 * lax.axis_index("row") + lax.axis_index("col")
    return 2 * (n % 128) + n // 128


def arc_tangent(value):
    for _ in range(2):
        value = value / (1.0 + jnp.sqrt(1.0 + value * value))
    square = value * value
    total = 1.0 / 17.0
    for k in range(15, 0, -2):
        total = 1.0 / k - square * total
    return 4.0 * value * total


def columns_kernel(
    fresnel_ref,
    terms_ref,
    field_ref,
    mats_ref,
    ahead_ref,
    behind_ref,
    spin_ref,
    out_ref,
    work_ref,
    back_ref,
):
    device = device_number()
    quad, group = device // 32, device % 32
    sub = lax.broadcasted_iota(jnp.int32, (8, 128), 0)
    lane = lax.broadcasted_iota(jnp.int32, (8, 128), 1)
    first = (sub & 2) == 0
    sign = jnp.where(first, 1.0, -1.0).astype(F32)

    def shift(value, amount, axis):
        return pltpu.roll(value, amount, axis + value.ndim - 2)

    def swap_pairs(value):
        return jnp.where(first, shift(value, 6, 0), shift(value, 2, 0))

    for nb in range(8):
        lines = []
        for na in range(16):
            n = 8 * na + nb
            one, two = field_ref[2 * n], field_ref[2 * n + 1]
            one, two = one + two, one - two
            line = (jnp.where(first, one, shift(two, 2, 0)), jnp.where(first, shift(one, 6, 0), two))
            if n:
                angle = 2.0 * math.pi * n / 256
                line = times(
                    line,
                    jnp.where(first, 1.0, math.cos(angle)).astype(F32),
                    jnp.where(first, 0.0, -math.sin(angle)).astype(F32),
                )
            lines.append(line)
        for ka, line in enumerate(transform(lines, -1)):
            real, imag = turned(line, nb * ka, 128, -1)
            work_ref[0, ka, nb] = real
            work_ref[1, ka, nb] = imag

    slot = ((lane >> 4) & 3) ^ (2 * (quad & 1))
    s = ((sub >> 2) << 1) | (sub & 1)
    positive = 4 * group + s
    base = 2 * group + (s & 1)
    mirrored = jnp.where(s < 2, base, jnp.where(base == 0, 64, 128 - base))
    halfway = jnp.where(s < 2, base, 127 - base)
    k2 = jnp.where(slot < 2, positive, 127 - positive)
    k1 = 2 * quad + (slot & 1)
    k1 = jnp.where(slot < 2, k1, 32 - k1)
    special = (quad == 0) & ((slot & 1) == 0)
    k2 = jnp.where(special, jnp.where(slot == 0, mirrored, halfway), k2)
    k1 = jnp.where(special, jnp.where(slot == 0, 0, 16), k1)
    v = k1 + 32 * k2
    v = jnp.where(v >= N // 2, v - N, v).astype(F32)
    v_square = v * v
    a2 = lane & 15
    u_base = (((sub >> 1) & 1) + 256 * a2 - jnp.where(a2 >= 8, N, 0)).astype(F32)
    later = lane >= 64
    rate_even = (0.5 / (N * N)) / jnp.where(later, fresnel_ref[2], fresnel_ref[0])
    rate_odd = (0.5 / (N * N)) / jnp.where(later, fresnel_ref[3], fresnel_ref[1])
    ratio = jnp.full((8, 128), terms_ref[0], F32)
    offset = arc_tangent(ratio) * (0.5 / math.pi)
    gain = 2.0 * jnp.sqrt(1.0 + ratio * ratio)
    floor = terms_ref[1] / gain

    def rows_of(table, which, start, count, stride):
        picked = []
        for part in range(2):
            tiles = []
            for k in range(count):
                at = pl.ds(start + stride * k, 1)
                upper = jnp.broadcast_to(table[which + (part, 0, at)], (8, 128))
                lower = jnp.broadcast_to(table[which + (part, 1, at)], (8, 128))
                tiles.append(jnp.where(first, upper, lower))
            picked.append(jnp.stack(tiles))
        return picked

    forward = (mats_ref[0], mats_ref[1])
    inverse = (mats_ref[2], mats_ref[3])
    natural = ((1,), (0,))
    for bunch in range(4):
        reals, imags = [], []
        for ka in range(4 * bunch, 4 * bunch + 4):
            lines = transform([(work_ref[0, ka, nb], work_ref[1, ka, nb]) for nb in range(8)], -1)
            real = jnp.stack([z[0] for z in lines])
            imag = jnp.stack([z[1] for z in lines])
            cosine, sine = (
                jnp.stack([ahead_ref[part, ka + 16 * kb] for kb in range(8)]) for part in range(2)
            )
            real, imag = times((real, imag), cosine, -sine)
            reals.append(real.reshape(64, 128))
            imags.append(imag.reshape(64, 128))
        mixed = jnp.concatenate(
            [jnp.concatenate(reals, 0), jnp.concatenate(imags, 0)], 1
        )
        mixed = product(split(mixed), forward, natural)
        reals, imags = [], []
        for step in range(4):
            ka = 4 * bunch + step
            rows = slice(64 * step, 64 * step + 64)
            real = mixed[rows, :128].reshape(8, 8, 128)
            imag = mixed[rows, 128:].reshape(8, 8, 128)
            for kb in range(8):
                u = u_base + float(2 * ka + 32 * kb)
                radius = u * u + v_square
                even = sine_turns(radius * rate_even + offset)
                odd = sine_turns(radius * rate_odd + offset)
                energy = even * even + odd * odd
                scale = 1.0 / (gain * (energy + shift(energy, 64, 1)) + floor)
                reals.append((even * real[kb] + odd * imag[kb]) * scale)
                imags.append((even * imag[kb] - odd * real[kb]) * scale)
        mixed = jnp.concatenate(
            [jnp.concatenate(reals, 0), jnp.concatenate(imags, 0)], 1
        )
        mixed = product(split(mixed), inverse, natural)
        for step in range(4):
            ka = 4 * bunch + step
            rows = slice(64 * step, 64 * step + 64)
            real = mixed[rows, :128].reshape(8, 8, 128)
            imag = mixed[rows, 128:].reshape(8, 8, 128)
            early = times((real[:4], imag[:4]), *rows_of(behind_ref, (0,), ka, 4, 16))
            later_half = times((real[4:], imag[4:]), *rows_of(behind_ref, (1,), ka, 4, 16))
            real, imag = plus(early, later_half)
            back_ref[0, ka] = real
            back_ref[1, ka] = imag

    for wb in range(8):
        lines = [
            tuple(back_ref[part, wb + 8 * (wa % 2), wa // 2] for part in range(2)) for wa in range(8)
        ]
        for na, line in enumerate(transform(lines, 1)):
            real, imag = turned(line, wb * na, 64, 1)
            work_ref[0, na, wb] = real
            work_ref[1, na, wb] = imag
    bit5 = (lane & 32) != 0
    reflected = (quad == 0) & ((lane & 16) == 0)
    itself = (quad == 0) & (group == 0) & ((lane & 48) == 0) & ((sub & 1) == 0)
    low_half = (lane & 8) == 0
    straight = ((sub & 4) != 0) == (lane >= 64)

    def partner(value):
        across = jnp.where(bit5, shift(value, 32, 1), shift(value, 96, 1))
        down = jnp.where(itself, value, shift(value, 4, 0))
        return jnp.where(reflected, down, across)

    for na in range(8):
        lines = [(work_ref[0, na, wb], work_ref[1, na, wb]) for wb in range(8)]
        for nb, line in enumerate(transform(lines, 1)):
            at = pl.ds(na + 8 * nb, 1)
            cosine, sine = (jnp.broadcast_to(spin_ref[part, at], (8, 128)) for part in range(2))
            line = times(line, jnp.where(first, 1.0, cosine), jnp.where(first, 0.0, sine))
            real, imag = (swap_pairs(z) + sign * z for z in line)
            real, imag = real + partner(real), imag - partner(imag)
            packed = real + jnp.where(low_half, -shift(imag, 120, 1), shift(imag, 8, 1))
            crossed = shift(shift(packed, 64, 1), 4, 0)
            out_ref[na + 8 * nb] = jnp.where(straight, packed, crossed)


def image_kernel(field_ref, mats_ref, twist_ref, out_ref):
    lane = lax.broadcasted_iota(jnp.int32, (64, 128), 1)
    bit6, bit3 = (lane & 64) != 0, (lane & 8) != 0
    tiles = {}
    for half in range(2):
        quads = [field_ref[pl.ds(256 * half + 64 * q, 64), :] for q in range(4)]
        parts = []
        for qb in range(2):
            one, two = quads[qb], quads[2 + qb]
            parts.append(
                (
                    jnp.where(bit6, pltpu.roll(two, 64, 1), one),
                    jnp.where(bit6, two, pltpu.roll(one, 64, 1)),
                )
            )
        stacked = []
        for s1 in range(2):
            one, two = parts[0][s1], parts[1][s1]
            stacked.append(jnp.where(bit3, pltpu.roll(two, 8, 1), one))
            stacked.append(jnp.where(bit3, two, pltpu.roll(one, 120, 1)))
        lines = jnp.concatenate(stacked, 0).T
        for q in range(4):
            for slot, k1 in enumerate(residues(4 * half + q)):
                start = 64 * (q // 2) + 16 * slot + 8 * (q % 2)
                tiles[k1] = lines[start : start + 8]
    lines = {}
    for kind, members in (
        (POS, [1, *range(1, 16)]),
        (NEG, [17, *range(17, 32)]),
        (ZERO, [0, 0]),
        (HALF, [16, 16]),
    ):
        data = split(jnp.concatenate([tiles[k1] for k1 in members], 0))
        value = product(data, (mats_ref[kind, 0], mats_ref[kind, 1]), ((1,), (0,)))
        for k, k1 in enumerate(members):
            line = (value[8 * k : 8 * k + 8, :128], value[8 * k : 8 * k + 8, 128:])
            lines[k1] = times(line, twist_ref[0, pl.ds(k1, 1), :], twist_ref[1, pl.ds(k1, 1), :])
    for n1, (real, imag) in enumerate(transform([lines[k1] for k1 in range(32)], 1)):
        at = pl.ds(128 * (n1 % 4), 128)
        out_ref[n1 // 4, pl.ds(0, 8), at] = real
        out_ref[n1 // 4, pl.ds(8, 8), at] = imag


def call(kernel, out_shape, scratch, arguments, spaces):
    return pl.pallas_call(
        kernel,
        out_shape=jax.ShapeDtypeStruct(out_shape, F32),
        in_specs=[pl.BlockSpec(memory_space=space) for space in spaces],
        out_specs=pl.BlockSpec(memory_space=pltpu.VMEM),
        scratch_shapes=scratch,
        compiler_params=pltpu.CompilerParams(vmem_limit_bytes=40 * 1024 * 1024),
    )(*arguments)


def image_rows(chunks):
    arguments = chunks + [jnp.asarray(c) for c in row_constants()]
    scratch = [pltpu.VMEM((1024, 256), BF16), pltpu.VMEM((1024, 256), BF16)]
    scratch.append(pltpu.VMEM((8, 4, 16, 512), F32))
    return call(rows_kernel, (256, 8, 128), scratch, arguments, [pltpu.VMEM] * 10)


def filter_columns(field, fresnel, ctf_terms):
    constants = [jnp.asarray(c) for c in column_constants()]
    scratch = [pltpu.VMEM((2, 16, 8, 8, 128), F32), pltpu.VMEM((2, 16, 4, 8, 128), F32)]
    spaces = [pltpu.SMEM] * 2 + [pltpu.VMEM] * 5
    arguments = [fresnel, ctf_terms, field] + constants
    return call(columns_kernel, (64, 8, 128), scratch, arguments, spaces)


def image_from(field):
    arguments = [field] + [jnp.asarray(c) for c in image_constants()]
    return call(image_kernel, (8, 16, 512), [], arguments, [pltpu.VMEM] * 3)


STEPS = [(2, 1), (0, 1), (2, 0), (1, 1), (3, 0), (3, 1), (1, 0)]


def there(place, step, flip):
    return (place // 4 ^ flip) * 4 + (place + step + 4) % 4


def ring_exchange(field):
    me = lax.axis_index("col")
    chunks = []
    for step, flip in STEPS:
        chunk = lax.dynamic_slice_in_dim(field, there(me, step, flip), 1, 1)
        pairs = [(place, there(place, step, flip)) for place in range(8)]
        chunks.append(lax.ppermute(chunk.reshape(4, 16, 512), "col", pairs))
    own = lax.dynamic_slice_in_dim(field, me, 1, 1)
    return chunks + [own.reshape(4, 16, 512)]


def exchange(field):
    return lax.all_to_all(field, "col", split_axis=0, concat_axis=0, tiled=True)


def exchange_all(field):
    return lax.all_to_all(
        field, ("row", "col"), split_axis=0, concat_axis=0, tiled=True, axis_index_groups=[ORDER]
    )


def local(holograms, fresnel, ctf_terms):
    field = image_rows(ring_exchange(holograms.reshape(4, 8, 16, 512)))
    field = filter_columns(exchange_all(field), fresnel, ctf_terms)
    field = exchange_all(field.reshape(256, 2, 128))
    image = image_from(field.reshape(512, 128))
    return exchange(image).reshape(128, 512)


def solution(mesh):
    in_specs = (P(None, "row", "col"), P(), P())
    out_specs = P("row", "col")
    return jax.shard_map(local, mesh=mesh, in_specs=in_specs, out_specs=out_specs, check_vma=False)
```

```python
import math

import jax
import jax.numpy as jnp
import ml_dtypes
import numpy as np
from jax import lax
from jax.experimental import pallas as pl
from jax.experimental.pallas import tpu as pltpu
from jax.sharding import PartitionSpec as P

N = 4096
POS, NEG, ZERO, HALF = range(4)
ORDER = [128 * (place % 2) + place // 2 for place in range(256)]
F32 = jnp.float32
BF16 = jnp.bfloat16


def residues(quad):
    low, high = 2 * quad, 2 * quad + 1
    if quad == 0:
        return [0, 1, 16, 31]
    if quad % 2:
        return [32 - low, 32 - high, low, high]
    return [low, high, 32 - low, 32 - high]


def member(kind, group, slot):
    if kind == POS:
        return 4 * group + slot
    if kind == NEG:
        return 127 - 4 * group - slot
    if kind == ZERO:
        return [2 * group, 2 * group + 1, 128 - 2 * group if group else 64, 127 - 2 * group][slot]
    return [2 * group, 2 * group + 1, 127 - 2 * group, 126 - 2 * group][slot]


def halves(matrix):
    high = matrix.astype(ml_dtypes.bfloat16)
    low = (matrix - high.astype(np.float64)).astype(ml_dtypes.bfloat16)
    return np.stack([high, low])


def turn(product, length):
    angle = 2.0 * np.pi * (np.asarray(product, np.int64) % length) / length
    return np.cos(angle), np.sin(angle)


def line_twist():
    return np.stack(turn(np.arange(32)[:, None] * np.arange(128), N)).astype(np.float32)


def row_constants():
    mats = []
    for kind in range(4):
        k2 = np.array([[member(kind, g, s) for s in range(4)] for g in range(32)])
        cosine, sine = turn(k2[:, :, None] * np.arange(128), 128)
        real = np.concatenate([cosine, sine], -1)
        imag = np.concatenate([-sine, cosine], -1)
        both = np.stack([real.reshape(32, 2, 2, 256), imag.reshape(32, 2, 2, 256)], 2)
        mats.append(halves(both.reshape(256, 256)))
    return np.stack(mats), line_twist()


def column_constants():
    cosine, sine = turn(np.arange(16)[:, None] * np.arange(16), 16)
    eye8 = np.eye(8)
    forward = np.block(
        [
            [np.kron(eye8, cosine), np.kron(eye8, -sine)],
            [np.kron(eye8, sine), np.kron(eye8, cosine)],
        ]
    )
    pick = np.kron(np.ones((2, 2)), np.eye(4))

    def spread(block):
        return np.kron(pick, block)

    inverse = np.block([[spread(cosine), spread(sine)], [spread(-sine), spread(cosine)]])
    lane = np.arange(128)
    within = lane % 16
    top = lane // 64
    parity = np.arange(2)[:, None, None]
    ahead = np.stack(turn((2 * np.arange(128)[None, :, None] + parity) * within, N))
    steps = np.arange(64)[None, :, None]
    behind = [
        turn((2 * steps + parity + 128 * h) * within + (32 * steps + 2048 * h) * top, N)
        for h in range(2)
    ]
    spin = np.stack(turn(2 * np.arange(64)[:, None] + top, 256)).astype(np.float32)
    ahead = np.repeat(ahead[:, [0, 1, 0, 1]].transpose(0, 2, 1, 3), 2, 2)
    ahead, behind = ahead.astype(np.float32), np.stack(behind).astype(np.float32)
    return np.concatenate([halves(forward), halves(inverse)]), ahead, behind, spin


def image_constants():
    mats = []
    for kind in range(4):
        k2 = np.array([[member(kind, g, s) for g in range(32)] for s in range(4)])
        k2 = k2.reshape(2, 2, 32).transpose(0, 2, 1).reshape(2, 64)
        cosine, sine = turn(k2[:, :, None] * np.arange(128), 128)
        real = np.concatenate([cosine, sine], -1)
        imag = np.concatenate([-sine, cosine], -1)
        mats.append(halves(np.stack([real, imag], 1).reshape(256, 256) * (0.5 / (N * N))))
    return np.stack(mats), line_twist()


def turned(value, angle_index, length, sign):
    angle_index %= length
    real, imag = value
    if angle_index == 0:
        return value
    if 4 * angle_index == length:
        return (-imag, real) if sign > 0 else (imag, -real)
    if 2 * angle_index == length:
        return (-real, -imag)
    if 4 * angle_index == 3 * length:
        return (imag, -real) if sign > 0 else (-imag, real)
    angle = sign * 2.0 * math.pi * angle_index / length
    cosine, sine = math.cos(angle), math.sin(angle)
    if (8 * angle_index) % length == 0:
        scale = abs(cosine)
        plus, minus = (real + imag) * scale, (real - imag) * scale
        if cosine > 0:
            return (minus, plus) if sine > 0 else (plus, -minus)
        return (-plus, minus) if sine > 0 else (-minus, -plus)
    return (real * cosine - imag * sine, imag * cosine + real * sine)


def plus(a, b):
    return (a[0] + b[0], a[1] + b[1])


def minus(a, b):
    return (a[0] - b[0], a[1] - b[1])


def transform(values, sign):
    length = len(values)
    if length == 1:
        return values
    if length == 2:
        return [plus(values[0], values[1]), minus(values[0], values[1])]
    quarter = length // 4
    columns = []
    for b in range(quarter):
        z0, z1, z2, z3 = (values[a * quarter + b] for a in range(4))
        even, odd = plus(z0, z2), plus(z1, z3)
        even_gap, odd_gap = minus(z0, z2), turned(minus(z1, z3), 1, 4, sign)
        outs = [plus(even, odd), plus(even_gap, odd_gap), minus(even, odd), minus(even_gap, odd_gap)]
        columns.append([turned(z, b * k, length, sign) for k, z in enumerate(outs)])
    result = [None] * length
    for k in range(4):
        for m, z in enumerate(transform([columns[b][k] for b in range(quarter)], sign)):
            result[k + 4 * m] = z
    return result


def times(value, cosine, sine):
    real, imag = value
    return (real * cosine - imag * sine, imag * cosine + real * sine)


def split(value):
    high = value.astype(BF16)
    return high, (value - high.astype(F32)).astype(BF16)


def product(left, right, dims):
    def one(a, b):
        return lax.dot_general(a, b, (dims, ((), ())), preferred_element_type=F32)

    return one(left[0], right[0]) + (one(left[0], right[1]) + one(left[1], right[0]))


def rows_kernel(*refs):
    chunk_refs = refs[:8]
    mats_ref, twist_ref, out_ref, high_ref, low_ref, field_ref = refs[8:]
    me = column_number()
    for (step, flip), chunk_ref in zip(STEPS + [(0, 0)], chunk_refs):
        field_ref[there(me, -step, flip)] = chunk_ref[...]
    for j in range(2):
        lines = []
        for n1 in range(32):
            at = pl.ds(128 * (n1 % 4), 128)
            lines.append(
                (field_ref[n1 // 4, 2 * j, :, at], field_ref[n1 // 4, 2 * j + 1, :, at])
            )
        lines = transform(lines, -1)
        for k1, line in enumerate(lines):
            if k1:
                line = times(line, twist_ref[0, pl.ds(k1, 1), :], -twist_ref[1, pl.ds(k1, 1), :])
            place = k1 if k1 < 16 else 16 + ((32 - k1) % 16 ^ 2)
            rows = pl.ds(128 * (place // 4) + 64 * j + 16 * (place % 4), 16)
            for part in range(2):
                high, low = split(line[part])
                high_ref[rows, pl.ds(128 * part, 128)] = high
                low_ref[rows, pl.ds(128 * part, 128)] = low

    def mixed(kind, start, count):
        rows = pl.ds(start, count)
        data = (high_ref[rows, :], low_ref[rows, :])
        return product((mats_ref[kind, 0], mats_ref[kind, 1]), data, ((1,), (1,)))

    lane = lax.broadcasted_iota(jnp.int32, (256, 128), 1)
    for half in range(2):
        positive, negative = mixed(POS, 256 * half, 256), mixed(NEG, 512 + 256 * half, 256)
        for pair in range(2):
            at = slice(128 * pair, 128 * pair + 128)
            one, two = positive[:, at], negative[:, at]
            low = (lane & 32) == 0
            even, odd = jnp.where(low, one, two), jnp.where(low, two, one)
            if half == 0 and pair == 0:
                even = jnp.where((lane & 48) == 0, mixed(ZERO, 0, 128), even)
                even = jnp.where((lane & 48) == 32, mixed(HALF, 512, 128), even)
            for side, block in enumerate([even, odd]):
                quad = 4 * half + 2 * pair + side
                out_ref[pl.ds(32 * quad, 32)] = block.reshape(32, 8, 128)


def sine_turns(turns):
    t = turns - jnp.round(turns)
    square = t * t
    total = SINE[-1]
    for coefficient in SINE[-2::-1]:
        total = total * square + coefficient
    return total * t


def sine_fit():
    nodes = np.cos(np.pi * (np.arange(400) + 0.5) / 800) * 0.5
    basis = np.stack([nodes ** (2 * k + 1) for k in range(6)], 1)
    return [float(c) for c in np.linalg.lstsq(basis, np.sin(2 * np.pi * nodes), rcond=None)[0]]


SINE = sine_fit()


def column_number():
    return lax.axis_index("col")


def device_number():
    n = 8 * lax.axis_index("row") + lax.axis_index("col")
    return 2 * (n % 128) + n // 128


def arc_tangent(value):
    for _ in range(2):
        value = value / (1.0 + jnp.sqrt(1.0 + value * value))
    square = value * value
    total = 1.0 / 17.0
    for k in range(15, 0, -2):
        total = 1.0 / k - square * total
    return 4.0 * value * total


def columns_kernel(
    fresnel_ref,
    terms_ref,
    field_ref,
    mats_ref,
    ahead_ref,
    behind_ref,
    spin_ref,
    out_ref,
    work_ref,
    back_ref,
):
    device = device_number()
    quad, group = device // 32, device % 32
    sub = lax.broadcasted_iota(jnp.int32, (8, 128), 0)
    lane = lax.broadcasted_iota(jnp.int32, (8, 128), 1)
    first = (sub & 2) == 0
    sign = jnp.where(first, 1.0, -1.0).astype(F32)

    def shift(value, amount, axis):
        return pltpu.roll(value, amount, axis + value.ndim - 2)

    def swap_pairs(value):
        return jnp.where(first, shift(value, 6, 0), shift(value, 2, 0))

    for nb in range(8):
        lines = []
        for na in range(16):
            n = 8 * na + nb
            one, two = field_ref[2 * n], field_ref[2 * n + 1]
            one, two = one + two, one - two
            line = (jnp.where(first, one, shift(two, 2, 0)), jnp.where(first, shift(one, 6, 0), two))
            if n:
                angle = 2.0 * math.pi * n / 256
                line = times(
                    line,
                    jnp.where(first, 1.0, math.cos(angle)).astype(F32),
                    jnp.where(first, 0.0, -math.sin(angle)).astype(F32),
                )
            lines.append(line)
        for ka, line in enumerate(transform(lines, -1)):
            real, imag = turned(line, nb * ka, 128, -1)
            work_ref[0, ka, nb] = real
            work_ref[1, ka, nb] = imag

    slot = ((lane >> 4) & 3) ^ (2 * (quad & 1))
    s = ((sub >> 2) << 1) | (sub & 1)
    positive = 4 * group + s
    base = 2 * group + (s & 1)
    mirrored = jnp.where(s < 2, base, jnp.where(base == 0, 64, 128 - base))
    halfway = jnp.where(s < 2, base, 127 - base)
    k2 = jnp.where(slot < 2, positive, 127 - positive)
    k1 = 2 * quad + (slot & 1)
    k1 = jnp.where(slot < 2, k1, 32 - k1)
    special = (quad == 0) & ((slot & 1) == 0)
    k2 = jnp.where(special, jnp.where(slot == 0, mirrored, halfway), k2)
    k1 = jnp.where(special, jnp.where(slot == 0, 0, 16), k1)
    v = k1 + 32 * k2
    v = jnp.where(v >= N // 2, v - N, v).astype(F32)
    v_square = v * v
    a2 = lane & 15
    u_base = (((sub >> 1) & 1) + 256 * a2 - jnp.where(a2 >= 8, N, 0)).astype(F32)
    later = lane >= 64
    rate_even = (0.5 / (N * N)) / jnp.where(later, fresnel_ref[2], fresnel_ref[0])
    rate_odd = (0.5 / (N * N)) / jnp.where(later, fresnel_ref[3], fresnel_ref[1])
    ratio = jnp.full((8, 128), terms_ref[0], F32)
    offset = arc_tangent(ratio) * (0.5 / math.pi)
    gain = 2.0 * jnp.sqrt(1.0 + ratio * ratio)
    floor = terms_ref[1] / gain

    def rows_of(table, which, start, count, stride):
        picked = []
        for part in range(2):
            tiles = []
            for k in range(count):
                at = pl.ds(start + stride * k, 1)
                upper = jnp.broadcast_to(table[which + (part, 0, at)], (8, 128))
                lower = jnp.broadcast_to(table[which + (part, 1, at)], (8, 128))
                tiles.append(jnp.where(first, upper, lower))
            picked.append(jnp.stack(tiles))
        return picked

    forward = (mats_ref[0], mats_ref[1])
    inverse = (mats_ref[2], mats_ref[3])
    natural = ((1,), (0,))
    for bunch in range(4):
        reals, imags = [], []
        for ka in range(4 * bunch, 4 * bunch + 4):
            lines = transform([(work_ref[0, ka, nb], work_ref[1, ka, nb]) for nb in range(8)], -1)
            real = jnp.stack([z[0] for z in lines])
            imag = jnp.stack([z[1] for z in lines])
            cosine, sine = (
                jnp.stack([ahead_ref[part, ka + 16 * kb] for kb in range(8)]) for part in range(2)
            )
            real, imag = times((real, imag), cosine, -sine)
            reals.append(real.reshape(64, 128))
            imags.append(imag.reshape(64, 128))
        mixed = jnp.concatenate(
            [jnp.concatenate(reals, 0), jnp.concatenate(imags, 0)], 1
        )
        mixed = product(split(mixed), forward, natural)
        reals, imags = [], []
        for step in range(4):
            ka = 4 * bunch + step
            rows = slice(64 * step, 64 * step + 64)
            real = mixed[rows, :128].reshape(8, 8, 128)
            imag = mixed[rows, 128:].reshape(8, 8, 128)
            for kb in range(8):
                u = u_base + float(2 * ka + 32 * kb)
                radius = u * u + v_square
                even = sine_turns(radius * rate_even + offset)
                odd = sine_turns(radius * rate_odd + offset)
                energy = even * even + odd * odd
                scale = 1.0 / (gain * (energy + shift(energy, 64, 1)) + floor)
                reals.append((even * real[kb] + odd * imag[kb]) * scale)
                imags.append((even * imag[kb] - odd * real[kb]) * scale)
        mixed = jnp.concatenate(
            [jnp.concatenate(reals, 0), jnp.concatenate(imags, 0)], 1
        )
        mixed = product(split(mixed), inverse, natural)
        for step in range(4):
            ka = 4 * bunch + step
            rows = slice(64 * step, 64 * step + 64)
            real = mixed[rows, :128].reshape(8, 8, 128)
            imag = mixed[rows, 128:].reshape(8, 8, 128)
            early = times((real[:4], imag[:4]), *rows_of(behind_ref, (0,), ka, 4, 16))
            later_half = times((real[4:], imag[4:]), *rows_of(behind_ref, (1,), ka, 4, 16))
            real, imag = plus(early, later_half)
            back_ref[0, ka] = real
            back_ref[1, ka] = imag

    for wb in range(8):
        lines = [
            tuple(back_ref[part, wb + 8 * (wa % 2), wa // 2] for part in range(2)) for wa in range(8)
        ]
        for na, line in enumerate(transform(lines, 1)):
            real, imag = turned(line, wb * na, 64, 1)
            work_ref[0, na, wb] = real
            work_ref[1, na, wb] = imag
    bit5 = (lane & 32) != 0
    reflected = (quad == 0) & ((lane & 16) == 0)
    itself = (quad == 0) & (group == 0) & ((lane & 48) == 0) & ((sub & 1) == 0)
    low_half = (lane & 8) == 0
    straight = ((sub & 4) != 0) == (lane >= 64)

    def partner(value):
        across = jnp.where(bit5, shift(value, 32, 1), shift(value, 96, 1))
        down = jnp.where(itself, value, shift(value, 4, 0))
        return jnp.where(reflected, down, across)

    for na in range(8):
        lines = [(work_ref[0, na, wb], work_ref[1, na, wb]) for wb in range(8)]
        for nb, line in enumerate(transform(lines, 1)):
            at = pl.ds(na + 8 * nb, 1)
            cosine, sine = (jnp.broadcast_to(spin_ref[part, at], (8, 128)) for part in range(2))
            line = times(line, jnp.where(first, 1.0, cosine), jnp.where(first, 0.0, sine))
            real, imag = (swap_pairs(z) + sign * z for z in line)
            real, imag = real + partner(real), imag - partner(imag)
            packed = real + jnp.where(low_half, -shift(imag, 120, 1), shift(imag, 8, 1))
            crossed = shift(shift(packed, 64, 1), 4, 0)
            out_ref[na + 8 * nb] = jnp.where(straight, packed, crossed)


def image_kernel(field_ref, mats_ref, twist_ref, out_ref):
    lane = lax.broadcasted_iota(jnp.int32, (64, 128), 1)
    bit6, bit3 = (lane & 64) != 0, (lane & 8) != 0
    tiles = {}
    for half in range(2):
        quads = [field_ref[pl.ds(256 * half + 64 * q, 64), :] for q in range(4)]
        parts = []
        for qb in range(2):
            one, two = quads[qb], quads[2 + qb]
            parts.append(
                (
                    jnp.where(bit6, pltpu.roll(two, 64, 1), one),
                    jnp.where(bit6, two, pltpu.roll(one, 64, 1)),
                )
            )
        stacked = []
        for s1 in range(2):
            one, two = parts[0][s1], parts[1][s1]
            stacked.append(jnp.where(bit3, pltpu.roll(two, 8, 1), one))
            stacked.append(jnp.where(bit3, two, pltpu.roll(one, 120, 1)))
        lines = jnp.concatenate(stacked, 0).T
        for q in range(4):
            for slot, k1 in enumerate(residues(4 * half + q)):
                start = 64 * (q // 2) + 16 * slot + 8 * (q % 2)
                tiles[k1] = lines[start : start + 8]
    lines = {}
    for kind, members in (
        (POS, [1, *range(1, 16)]),
        (NEG, [17, *range(17, 32)]),
        (ZERO, [0, 0]),
        (HALF, [16, 16]),
    ):
        data = split(jnp.concatenate([tiles[k1] for k1 in members], 0))
        value = product(data, (mats_ref[kind, 0], mats_ref[kind, 1]), ((1,), (0,)))
        for k, k1 in enumerate(members):
            line = (value[8 * k : 8 * k + 8, :128], value[8 * k : 8 * k + 8, 128:])
            lines[k1] = times(line, twist_ref[0, pl.ds(k1, 1), :], twist_ref[1, pl.ds(k1, 1), :])
    for n1, (real, imag) in enumerate(transform([lines[k1] for k1 in range(32)], 1)):
        at = pl.ds(128 * (n1 % 4), 128)
        out_ref[n1 // 4, pl.ds(0, 8), at] = real
        out_ref[n1 // 4, pl.ds(8, 8), at] = imag


def call(kernel, out_shape, scratch, arguments, spaces):
    return pl.pallas_call(
        kernel,
        out_shape=jax.ShapeDtypeStruct(out_shape, F32),
        in_specs=[pl.BlockSpec(memory_space=space) for space in spaces],
        out_specs=pl.BlockSpec(memory_space=pltpu.VMEM),
        scratch_shapes=scratch,
        compiler_params=pltpu.CompilerParams(vmem_limit_bytes=40 * 1024 * 1024),
    )(*arguments)


def image_rows(chunks):
    arguments = chunks + [jnp.asarray(c) for c in row_constants()]
    scratch = [pltpu.VMEM((1024, 256), BF16), pltpu.VMEM((1024, 256), BF16)]
    scratch.append(pltpu.VMEM((8, 4, 16, 512), F32))
    return call(rows_kernel, (256, 8, 128), scratch, arguments, [pltpu.VMEM] * 10)


def filter_columns(field, fresnel, ctf_terms):
    constants = [jnp.asarray(c) for c in column_constants()]
    scratch = [pltpu.VMEM((2, 16, 8, 8, 128), F32), pltpu.VMEM((2, 16, 4, 8, 128), F32)]
    spaces = [pltpu.SMEM] * 2 + [pltpu.VMEM] * 5
    arguments = [fresnel, ctf_terms, field] + constants
    return call(columns_kernel, (64, 8, 128), scratch, arguments, spaces)


def image_from(field):
    arguments = [field] + [jnp.asarray(c) for c in image_constants()]
    return call(image_kernel, (8, 16, 512), [], arguments, [pltpu.VMEM] * 3)


STEPS = [(1, 0), (3, 1), (3, 0), (1, 1), (2, 0), (0, 1), (2, 1)]


def there(place, step, flip):
    return (place // 4 ^ flip) * 4 + (place + step + 4) % 4


def ring_exchange(field):
    me = lax.axis_index("col")
    chunks = []
    for step, flip in STEPS:
        chunk = lax.dynamic_slice_in_dim(field, there(me, step, flip), 1, 1)
        pairs = [(place, there(place, step, flip)) for place in range(8)]
        chunks.append(lax.ppermute(chunk.reshape(4, 16, 512), "col", pairs))
    own = lax.dynamic_slice_in_dim(field, me, 1, 1)
    return chunks + [own.reshape(4, 16, 512)]


def exchange(field):
    return lax.all_to_all(field, "col", split_axis=0, concat_axis=0, tiled=True)


def exchange_all(field):
    return lax.all_to_all(
        field, ("row", "col"), split_axis=0, concat_axis=0, tiled=True, axis_index_groups=[ORDER]
    )


def local(holograms, fresnel, ctf_terms):
    field = image_rows(ring_exchange(holograms.reshape(4, 8, 16, 512)))
    field = filter_columns(exchange_all(field), fresnel, ctf_terms)
    field = exchange_all(field.reshape(256, 2, 128))
    image = image_from(field.reshape(512, 128))
    return exchange(image).reshape(128, 512)


def solution(mesh):
    in_specs = (P(None, "row", "col"), P(), P())
    out_specs = P("row", "col")
    return jax.shard_map(local, mesh=mesh, in_specs=in_specs, out_specs=out_specs, check_vma=False)
```
